256 devices in a mesh: slab: 32 (over z, y), lat: 8 (over x, core).
Axes of the slice: x: 4, y: 4, z: 8, core: 2. Of those that a mesh axis runs over, the one named last changes fastest.
Arguments:
- density: float32 [128, 512, 1024], P('slab', 'lat'), may hold values from 0.05 to 2
- bins: int32 [128, 512, 1024], P('slab', 'lat'), may hold values from 0 to 255
- transfer: bfloat16 [4, 256], replicated, may hold values from 0.099609375 to 1.5
- depth_order: int32 [512, 1024], P('lat'), may hold values 0 or 1
Outputs:
- frame: float32 [4, 512, 1024], P(None, ('lat', 'slab'))
The draws below stay inside these ranges and needn't reach their ends.
All inputs are finite; a program needn't handle non-finite values. No bound on the sum of `depth_order` on one device may be relied on, other than what follows from the above.
Results may differ from the reference program's by a relative error of at most 0.0003.
Values sent between devices are 32-bit elements; how exact they have to be, the bound alone decides.
No kernel may reach another device: no remote copies, remote signals or barrier semaphores. Data moves between devices by JAX's collectives and lax.ppermute only.
A program may use at most 64 MiB of HBM per device.

```python
import math
import jax
import jax.numpy as jnp
from jax import lax

CY = 64
CX = 1024
NBINS = 256
NZ = 128
NY = 512
N_LAT = 8


def touch_ends(result, rng, least, largest):
    dims = result.shape
    place = [jax.random.randint(jax.random.fold_in(rng, axis), (), 0, dims[axis]) for axis in range(len(dims))]
    result = result.at[tuple(place)].set(least)
    longest = dims.index(max(dims))
    place[longest] = (place[longest] + 1) % dims[longest]
    return result.at[tuple(place)].set(largest)


def level_of(rng, extent, cuts, smallest, top_value):
    def one(dim, shards_of):
        heights = jax.random.uniform(jax.random.fold_in(jax.random.fold_in(rng, 6), dim), (shards_of,), jnp.float32, smallest / len(cuts), top_value / len(cuts))
        return jnp.repeat(jnp.exp(heights), extent[dim] // shards_of).reshape((-1,) + (1,) * (len(extent) - dim - 1))

    loudness = one(*cuts[0])
    for cut in cuts[1:]:
        loudness = loudness * one(*cut)
    return loudness


def setup_inputs(seed: int = 0) -> dict:
    key_list = jax.random.split(jax.random.key(seed), 5)
    return {
        "density": jnp.clip(jnp.exp(math.log(2.0) - 3.6888794 * jax.random.uniform(key_list[0], (NZ, NY, CX), jnp.float32) ** level_of(key_list[0], (NZ, NY, CX), ((0, 32), (1, 8)), -0.2, 0.2)), 0.05, 2.0),
        "bins": touch_ends(jax.random.randint(key_list[1], (NZ, NY, CX), 0, NBINS), jax.random.fold_in(key_list[1], 1), 0, NBINS - 1).astype(jnp.int32),
        "transfer": jnp.clip(jax.random.uniform(key_list[2], (4, NBINS), jnp.float32, 0.099609375, 1.5), 0.099609375, 1.5).astype(jnp.bfloat16),
        "depth_order": touch_ends((jax.random.randint(key_list[3], (NY, CX), 0, 2) < 1).astype(jnp.int32), jax.random.fold_in(key_list[3], 1), 0, 1),
    }


LIGHT_X = 0.48
LIGHT_Y = 0.6
LIGHT_Z = 0.64

def shading_of(padded):
    center = padded[1:-1, 1:-1, 1:-1]
    slope_z = (padded[2:, 1:-1, 1:-1] - padded[:-2, 1:-1, 1:-1]) * 0.5
    slope_y = (padded[1:-1, 2:, 1:-1] - padded[1:-1, :-2, 1:-1]) * 0.5
    slope_x = (padded[1:-1, 1:-1, 2:] - padded[1:-1, 1:-1, :-2]) * 0.5
    facing = LIGHT_X * slope_x + LIGHT_Y * slope_y + LIGHT_Z * slope_z
    shading = 1.0 + facing / jnp.sqrt(slope_x * slope_x + slope_y * slope_y + slope_z * slope_z + 0.25)
    return (center, shading)

def march(optical, radiance):
    running = jnp.cumsum(optical, axis=0)
    overall = running[-1]
    ahead = jnp.exp(optical - running)
    behind = jnp.exp(running - overall)
    front_rgb = lax.optimization_barrier(jnp.sum(radiance * ahead[None], axis=1))
    back_rgb = lax.optimization_barrier(jnp.sum(radiance * behind[None], axis=1))
    return (front_rgb, back_rgb, overall)

def reference(density, bins, transfer, depth_order):
    padded = jnp.pad(density, 1)
    lookup_table = transfer.astype(jnp.float32)
    spacing = 1.5 / NZ

    def one_block(index):
        start = index * CY
        padded_block = lax.dynamic_slice_in_dim(padded, start, CY + 2, 1)
        bins_block = lax.dynamic_slice_in_dim(bins, start, CY, 1)
        order_block = lax.dynamic_slice_in_dim(depth_order, start, CY, 0)
        center, shading = shading_of(padded_block)
        emission = jnp.take(lookup_table[0:3], bins_block, axis=1)
        extinction = jnp.take(lookup_table[3], bins_block)
        optical = extinction * center * spacing
        radiance = emission * (shading * (1.0 - jnp.exp(-optical)))[None]
        front_rgb, back_rgb, overall = march(optical, radiance)
        colors = jnp.where(order_block[None] == 1, back_rgb, front_rgb)
        opacity = 1.0 - jnp.exp(-overall)
        return jnp.concatenate([colors, opacity[None]], axis=0)
    blocks = lax.map(one_block, jnp.arange(N_LAT, dtype=jnp.int32))
    return jnp.transpose(blocks, (1, 0, 2, 3)).reshape(4, NY, CX)
```

```python
import jax
import jax.numpy as jnp
from jax import lax
from jax.experimental import pallas as pl
from jax.experimental.pallas import tpu as pltpu
from jax.sharding import PartitionSpec as P

LIGHT_X = 0.48
LIGHT_Y = 0.6
LIGHT_Z = 0.64
UNIT = 2048.0
LANES = 128
VMEM_LIMIT = 48 * 1024 * 1024
F32 = jnp.float32


def params():
    return pltpu.CompilerParams(vmem_limit_bytes=VMEM_LIMIT)


def faces_kernel(d_ref, za_ref, zb_ref, ya_ref, yb_ref, low, high, sems):
    depth, rows = d_ref.shape[0], d_ref.shape[1]
    slab_odd = lax.axis_index("slab") & 1
    lat_odd = lax.axis_index("lat") & 1
    last = depth - 1
    copies = [
        pltpu.make_async_copy(d_ref.at[:, pl.ds(0, 8)], low, sems.at[0]),
        pltpu.make_async_copy(d_ref.at[:, pl.ds(rows - 8, 8)], high, sems.at[1]),
        pltpu.make_async_copy(d_ref.at[last - last * slab_odd], za_ref, sems.at[2]),
        pltpu.make_async_copy(d_ref.at[last * slab_odd], zb_ref, sems.at[3]),
    ]
    for copy in copies:
        copy.start()
    copies[0].wait()
    copies[1].wait()
    odd = lat_odd == 1
    for k in range(depth):
        first, final = low[k, 0:1], high[k, 7:8]
        ya_ref[k : k + 1, :] = jnp.where(odd, first, final)
        yb_ref[k : k + 1, :] = jnp.where(odd, final, first)
    copies[2].wait()
    copies[3].wait()


def faces(density):
    depth, rows, line = density.shape
    return pl.pallas_call(
        faces_kernel,
        out_shape=[
            jax.ShapeDtypeStruct((rows, line), F32),
            jax.ShapeDtypeStruct((rows, line), F32),
            jax.ShapeDtypeStruct((depth, line), F32),
            jax.ShapeDtypeStruct((depth, line), F32),
        ],
        in_specs=[pl.BlockSpec(memory_space=pl.ANY)],
        out_specs=[pl.BlockSpec(memory_space=pl.ANY)] * 2
        + [pl.BlockSpec(memory_space=pltpu.VMEM)] * 2,
        scratch_shapes=[
            pltpu.VMEM((depth, 8, line), F32),
            pltpu.VMEM((depth, 8, line), F32),
            pltpu.SemaphoreType.DMA((4,)),
        ],
        compiler_params=params(),
        name="faces",
    )(density)


def look_up(table, bins):
    column = bins & (LANES - 1)
    upper = bins >= LANES
    words = []
    for low_half, high_half in table:
        a = jnp.take_along_axis(low_half, column, axis=1, mode="promise_in_bounds")
        b = jnp.take_along_axis(high_half, column, axis=1, mode="promise_in_bounds")
        words.append(jnp.where(upper, b, a))
    values = []
    for word in words:
        values += [(word & 0xFFFF).astype(F32), (word >> 16).astype(F32)]
    return values


def packed_table(t_ref):
    units = (t_ref[...].astype(F32) * UNIT).astype(jnp.int32)
    table = []
    for pair in range(2):
        word = units[2 * pair : 2 * pair + 1] | (units[2 * pair + 1 : 2 * pair + 2] << 16)
        table.append(
            [jnp.broadcast_to(word[:, h * LANES : (h + 1) * LANES], (8, LANES)) for h in range(2)]
        )
    return table


def cells_kernel(
    spacing, d_hbm, b_ref, t_ref, o_ref, ya_ref, yb_ref, c_ref, w_ref, a_ref, n_ref, d, sem
):
    depth, rows, line = d_hbm.shape
    chunks = line // LANES
    copy = pltpu.make_async_copy(d_hbm, d.at[:, pl.ds(8, rows)], sem)
    copy.start()
    lat = lax.axis_index("lat")
    lat_odd = (lat & 1) == 1
    keep_low = jnp.where(lat == 0, 0.0, 1.0).astype(F32)
    keep_high = jnp.where(lat == lax.axis_size("lat") - 1, 0.0, 1.0).astype(F32)
    table = packed_table(t_ref)
    for k in range(depth):
        from_a, from_b = ya_ref[k : k + 1, :], yb_ref[k : k + 1, :]
        d[k, 7:8, :] = jnp.where(lat_odd, from_a, from_b) * keep_low
        d[k, rows + 8 : rows + 9, :] = jnp.where(lat_odd, from_b, from_a) * keep_high
    lane = lax.broadcasted_iota(jnp.int32, (8, LANES), 1)
    sub = lax.broadcasted_iota(jnp.int32, (8, LANES), 0)
    first_lane, last_lane = lane == 0, lane == LANES - 1
    first_sub, last_sub = sub == 0, sub == 7
    scale = spacing / UNIT
    copy.wait()

    def tile(t, carry):
        base = pl.multiple_of(t * 8, 8)
        for c in range(chunks):
            cols = slice(c * LANES, (c + 1) * LANES)

            def cell(k, row, column=c):
                return d[k, pl.ds(row, 8), column * LANES : (column + 1) * LANES]

            reverse = o_ref[pl.ds(base, 8), cols] == 1
            passed, colors, tilt, norm = [], [], [], []
            for k in range(depth):
                here = cell(k, base + 8)
                before, after = cell(k, base), cell(k, base + 16)
                left = cell(k, base + 8, c - 1) if c > 0 else jnp.zeros_like(here)
                right = cell(k, base + 8, c + 1) if c < chunks - 1 else jnp.zeros_like(here)
                step_x = pltpu.roll(jnp.where(first_lane, right, here), LANES - 1, 1) - pltpu.roll(
                    jnp.where(last_lane, left, here), 1, 1
                )
                step_y = pltpu.roll(jnp.where(first_sub, after, here), 7, 0) - pltpu.roll(
                    jnp.where(last_sub, before, here), 1, 0
                )
                tilt.append(LIGHT_X * step_x + LIGHT_Y * step_y)
                norm.append(step_x * step_x + step_y * step_y + 1.0)
                red, green, blue, extinction = look_up(table, b_ref[k, pl.ds(base, 8), cols])
                passed.append(jnp.exp(-(extinction * scale * here)))
                colors.append((red, green, blue))
            t0, t1, t2, t3 = passed
            front, back = t0 * t1, t2 * t3
            ahead = [
                jnp.where(reverse, t1 * back, 1.0),
                jnp.where(reverse, back, t0),
                jnp.where(reverse, t3, front),
                jnp.where(reverse, 1.0, front * t2),
            ]
            total = [None, None, None]
            for k in range(depth):
                weight = (1.0 - passed[k]) * (1.0 / UNIT) * ahead[k]
                if k in (0, depth - 1):
                    edge = 0 if k == 0 else 1
                    for i in range(3):
                        w_ref[edge, i, pl.ds(base, 8), cols] = colors[k][i] * weight
                    a_ref[edge, pl.ds(base, 8), cols] = tilt[k]
                    n_ref[edge, pl.ds(base, 8), cols] = norm[k]
                    continue
                step_z = cell(k + 1, base + 8) - cell(k - 1, base + 8)
                shade = (tilt[k] + LIGHT_Z * step_z) * lax.rsqrt(norm[k] + step_z * step_z)
                weight = weight + weight * shade
                for i in range(3):
                    term = colors[k][i] * weight
                    total[i] = term if total[i] is None else total[i] + term
            for i in range(3):
                c_ref[i, pl.ds(base, 8), cols] = total[i]
            c_ref[3, pl.ds(base, 8), cols] = front * back
        return carry

    lax.fori_loop(0, rows // 8, tile, 0)


def cells(density, bins, transfer, order, ya, yb, spacing):
    depth, rows, line = density.shape
    vmem = pl.BlockSpec(memory_space=pltpu.VMEM)
    return pl.pallas_call(
        lambda *refs: cells_kernel(spacing, *refs),
        out_shape=[
            jax.ShapeDtypeStruct((4, rows, line), F32),
            jax.ShapeDtypeStruct((2, 3, rows, line), F32),
            jax.ShapeDtypeStruct((2, rows, line), F32),
            jax.ShapeDtypeStruct((2, rows, line), F32),
        ],
        in_specs=[pl.BlockSpec(memory_space=pl.ANY)] + [vmem] * 5,
        out_specs=[vmem] * 4,
        scratch_shapes=[pltpu.VMEM((depth, rows + 16, line), F32), pltpu.SemaphoreType.DMA],
        compiler_params=params(),
        cost_estimate=pl.CostEstimate(
            flops=100 * depth * rows * line, bytes_accessed=12 * depth * rows * line, transcendentals=2 * depth * rows * line
        ),
        name="cells",
    )(density, bins, transfer, order, ya, yb)


def swap_pieces(tiles, sub):
    for size in (4, 2):
        keep = (sub & size) == 0
        step = size // 2
        result = list(tiles)
        for i in range(4):
            if i & step == 0:
                a, b = tiles[i], tiles[i | step]
                result[i] = jnp.where(keep, a, pltpu.roll(b, size, 0))
                result[i | step] = jnp.where(keep, pltpu.roll(a, 8 - size, 0), b)
        tiles = result
    return tiles


def edges_kernel(d_ref, za_ref, zb_ref, o_ref, c_ref, w_ref, a_ref, n_ref, *rest):
    outs, mask_ref, s = rest[:8], rest[8], rest[9]
    depth, rows, line = d_ref.shape
    slab = lax.axis_index("slab")
    slab_odd = (slab & 1) == 1
    keep_low = jnp.where(slab == 0, 0.0, 1.0).astype(F32)
    keep_high = jnp.where(slab == lax.axis_size("slab") - 1, 0.0, 1.0).astype(F32)
    sub = lax.broadcasted_iota(jnp.int32, (8, LANES), 0)
    chunks = line // LANES

    def part(index, carry):
        half, c = index // chunks, index % chunks
        cols = pl.ds(pl.multiple_of(c * LANES, LANES), LANES)
        channels = [[] for _ in range(5)]
        for quarter in range(4):
            at = pl.ds(pl.multiple_of(16 * quarter + 8 * half, 8), 8)
            from_a, from_b = za_ref[at, cols], zb_ref[at, cols]
            below = jnp.where(slab_odd, from_a, from_b) * keep_low
            above = jnp.where(slab_odd, from_b, from_a) * keep_high
            total = [c_ref[i, at, cols] for i in range(3)]
            steps = (d_ref[1, at, cols] - below, above - d_ref[depth - 2, at, cols])
            for edge in range(2):
                step_z = steps[edge]
                shade = 1.0 + (a_ref[edge, at, cols] + LIGHT_Z * step_z) * lax.rsqrt(
                    n_ref[edge, at, cols] + step_z * step_z
                )
                for i in range(3):
                    total[i] = total[i] + w_ref[edge, i, at, cols] * shade
            for i in range(3):
                channels[i].append(total[i])
            channels[3].append(c_ref[3, at, cols])
            channels[4].append(o_ref[at, cols].astype(F32))
        for i in range(5):
            for piece, value in enumerate(swap_pieces(channels[i], sub)):
                s[4 * half + piece, i, :, cols] = value
        return carry

    lax.fori_loop(0, 2 * chunks, part, 0)
    place = slab & 7
    for j in range(8):
        for i in range(4):
            outs[j][i] = s[place ^ j, i]
    mask_ref[...] = s[place, 4]


def edges(density, za, zb, order, color, weight, tilt, norm):
    depth, rows, line = density.shape
    vmem = pl.BlockSpec(memory_space=pltpu.VMEM)
    return pl.pallas_call(
        edges_kernel,
        out_shape=[jax.ShapeDtypeStruct((4, 8, line), F32)] * 8
        + [jax.ShapeDtypeStruct((8, line), F32)],
        in_specs=[vmem] * 8,
        out_specs=[vmem] * 9,
        scratch_shapes=[pltpu.VMEM((8, 5, 8, line), F32)],
        compiler_params=params(),
        cost_estimate=pl.CostEstimate(
            flops=40 * depth * rows * line, bytes_accessed=4 * depth * rows * line, transcendentals=depth * rows * line
        ),
        name="edges",
    )(density, za, zb, order, color, weight, tilt, norm)


def merge(a, b, b_first):
    front = [jnp.where(b_first, y, x) for x, y in zip(a, b)]
    back = [jnp.where(b_first, x, y) for x, y in zip(a, b)]
    return [front[i] + front[3] * back[i] for i in range(3)] + [front[3] * back[3]]


def merge_tree(blocks, mask, place):
    bit = 0
    while len(blocks) > 1:
        b_first = jnp.logical_xor(mask > 0.5, (place >> bit & 1) == 1)
        blocks = [merge(blocks[i], blocks[i + 1], b_first) for i in range(0, len(blocks), 2)]
        bit += 1
    return blocks[0]


def eight_kernel(*refs):
    ins, mask_ref, outs, own_mask = refs[:8], refs[8], refs[9:13], refs[13]
    line = mask_ref.shape[1]
    slab = lax.axis_index("slab")
    place, quarter = slab & 7, slab >> 3
    sub = lax.broadcasted_iota(jnp.int32, (8, LANES), 0) // 2

    def part(c, carry):
        cols = pl.ds(pl.multiple_of(c * LANES, LANES), LANES)
        mask = mask_ref[:, cols]
        blocks = [[ref[i, :, cols] for i in range(4)] for ref in ins]
        merged = merge_tree(blocks, mask, place)
        for j in range(4):
            target = quarter ^ j
            packed = None
            for i in range(4):
                moved = pltpu.roll(merged[i], (2 * i + 8 - 2 * target) & 7, 0)
                packed = moved if packed is None else jnp.where(sub == i, moved, packed)
            outs[j][:, cols] = packed
        own_mask[:, cols] = pltpu.roll(mask, (8 - 2 * quarter) & 7, 0)
        return carry

    lax.fori_loop(0, line // LANES, part, 0)


def merge_eight(blocks, mask):
    line = mask.shape[1]
    vmem = pl.BlockSpec(memory_space=pltpu.VMEM)
    return pl.pallas_call(
        eight_kernel,
        out_shape=[jax.ShapeDtypeStruct((8, line), F32)] * 5,
        in_specs=[vmem] * 9,
        out_specs=[vmem] * 5,
        compiler_params=params(),
        name="merge_eight",
    )(*blocks, mask)


def four_kernel(*refs):
    ins, mask_ref, out = refs[:4], refs[4], refs[5]
    place = lax.axis_index("slab") >> 3
    mask = mask_ref[0:2, :]
    blocks = [[ref[2 * i : 2 * i + 2, :] for i in range(4)] for ref in ins]
    merged = merge_tree(blocks, mask, place)
    for i in range(3):
        out[i] = merged[i]
    out[3] = 1.0 - merged[3]


def merge_four(blocks, mask):
    line = mask.shape[1]
    vmem = pl.BlockSpec(memory_space=pltpu.VMEM)
    return pl.pallas_call(
        four_kernel,
        out_shape=jax.ShapeDtypeStruct((4, 2, line), F32),
        in_specs=[vmem] * 5,
        out_specs=vmem,
        compiler_params=params(),
        name="merge_four",
    )(*blocks, mask)


def swap(block, axis, step):
    count = lax.axis_size(axis)
    return lax.ppermute(block, axis, [(i, i ^ step) for i in range(count)])


def swap_odd(block, axis):
    count = lax.axis_size(axis)
    route = []
    for i in range(1, count, 2):
        route += [(i, (i + 1) % count), ((i + 1) % count, i)]
    return lax.ppermute(block, axis, route)


def shards(density, bins, transfer, depth_order):
    depth_cells = density.shape[0]
    spacing = 1.5 / (depth_cells * lax.axis_size("slab"))
    za, zb, ya, yb = faces(density)
    za, zb = swap(za, "slab", 1), swap_odd(zb, "slab")
    ya, yb = swap(ya, "lat", 1), swap_odd(yb, "lat")
    color, weight, tilt, norm = cells(density, bins, transfer, depth_order, ya, yb, spacing)
    *blocks, mask = edges(density, za, zb, depth_order, color, weight, tilt, norm)
    blocks = [blocks[0]] + [swap(blocks[j], "slab", j) for j in range(1, 8)]
    *quarters, mask = merge_eight(blocks, mask)
    quarters = [quarters[0]] + [swap(quarters[j], "slab", 8 * j) for j in range(1, 4)]
    return merge_four(quarters, mask)


def solution(mesh):
    return jax.shard_map(
        shards,
        mesh=mesh,
        in_specs=(P("slab", "lat", None), P("slab", "lat", None), P(), P("lat", None)),
        out_specs=P(None, ("lat", "slab"), None),
        check_vma=False,
    )
```

```python
import math

import jax
import jax.numpy as jnp
from jax import lax
from jax.experimental import pallas as pl
from jax.experimental.pallas import tpu as pltpu
from jax.sharding import PartitionSpec as P

LIGHT_X = 0.48
LIGHT_Y = 0.6
LIGHT_Z = 0.64
UNIT = 2048.0
LANES = 128
MIB = 1024 * 1024
F32 = jnp.float32
ORDER8 = (1, 7, 6, 5, 4, 3, 2, 0)
ORDER4 = (1, 2, 3, 0)


def params(mib):
    return pltpu.CompilerParams(vmem_limit_bytes=mib * MIB)


def faces_kernel(d_ref, t_ref, za_ref, zb_ref, ya_ref, yb_ref, table_ref, low, high, t, sems):
    depth, rows = d_ref.shape[0], d_ref.shape[1]
    slab_odd = lax.axis_index("slab") & 1
    lat_odd = lax.axis_index("lat") & 1
    last = depth - 1
    copies = [
        pltpu.make_async_copy(d_ref.at[last - last * slab_odd], za_ref, sems.at[0]),
        pltpu.make_async_copy(d_ref.at[last * slab_odd], zb_ref, sems.at[1]),
        pltpu.make_async_copy(d_ref.at[:, pl.ds(0, 8)], low, sems.at[2]),
        pltpu.make_async_copy(d_ref.at[:, pl.ds(rows - 8, 8)], high, sems.at[3]),
        pltpu.make_async_copy(t_ref, t, sems.at[4]),
    ]
    for copy in copies:
        copy.start()
    copies[4].wait()
    units = (t[...].astype(F32) * UNIT).astype(jnp.int32)
    for pair in range(2):
        word = units[2 * pair : 2 * pair + 1] | (units[2 * pair + 1 : 2 * pair + 2] << 16)
        for half in range(2):
            table_ref[2 * pair + half] = jnp.broadcast_to(
                word[:, half * LANES : (half + 1) * LANES], (8, LANES)
            )
    copies[2].wait()
    copies[3].wait()
    odd = lat_odd == 1
    for k in range(depth):
        first, final = low[k, 0:1], high[k, 7:8]
        ya_ref[k : k + 1, :] = jnp.where(odd, first, final)
        yb_ref[k : k + 1, :] = jnp.where(odd, final, first)
    copies[0].wait()
    copies[1].wait()


def faces(density, transfer):
    depth, rows, line = density.shape
    return pl.pallas_call(
        faces_kernel,
        out_shape=[
            jax.ShapeDtypeStruct((rows, line), F32),
            jax.ShapeDtypeStruct((rows, line), F32),
            jax.ShapeDtypeStruct((depth, line), F32),
            jax.ShapeDtypeStruct((depth, line), F32),
            jax.ShapeDtypeStruct((4, 8, LANES), jnp.int32),
        ],
        in_specs=[pl.BlockSpec(memory_space=pl.ANY)] * 2,
        out_specs=[pl.BlockSpec(memory_space=pl.ANY)] * 2
        + [pl.BlockSpec(memory_space=pltpu.VMEM)] * 3,
        scratch_shapes=[
            pltpu.VMEM((depth, 8, line), F32),
            pltpu.VMEM((depth, 8, line), F32),
            pltpu.VMEM(transfer.shape, transfer.dtype),
            pltpu.SemaphoreType.DMA((5,)),
        ],
        compiler_params=params(4),
        name="faces",
    )(density, transfer)


def columns_of(table, column):
    numbers = lax.GatherDimensionNumbers(
        offset_dims=(),
        collapsed_slice_dims=(1,),
        start_index_map=(1,),
        operand_batching_dims=(0,),
        start_indices_batching_dims=(0,),
    )
    return lax.gather(
        table, column[..., None], numbers, (1, 1), mode=lax.GatherScatterMode.PROMISE_IN_BOUNDS
    )


def look_up(table, bins):
    column = bins & (LANES - 1)
    upper = bins >= LANES
    values = []
    for low_half, high_half in table:
        word = jnp.where(upper, columns_of(high_half, column), columns_of(low_half, column))
        values += [(word & 0xFFFF).astype(F32), (word >> 16).astype(F32)]
    return values


def look_kernel(spacing, d_hbm, b_hbm, o_hbm, t_ref, d_ref, w_ref, l_ref, o_ref, b, sems):
    depth, rows, line = d_hbm.shape

    def copies(t):
        at = pl.ds(pl.multiple_of(t * 8, 8), 8)
        inner = pl.ds(pl.multiple_of(t * 8 + 8, 8), 8)
        return [
            pltpu.make_async_copy(b_hbm.at[:, at], b.at[:, at], sems.at[0, t]),
            pltpu.make_async_copy(d_hbm.at[:, at], d_ref.at[:, inner], sems.at[1, t]),
            pltpu.make_async_copy(o_hbm.at[at], o_ref.at[at], sems.at[2, t]),
        ]

    for t in range(rows // 8):
        for copy in copies(t):
            copy.start()
    table = [[t_ref[2 * pair + half] for half in range(2)] for pair in range(2)]
    scale = -spacing / (UNIT * math.log(2.0))

    def tile(t, carry):
        at = pl.ds(pl.multiple_of(t * 8, 8), 8)
        inner = pl.ds(pl.multiple_of(t * 8 + 8, 8), 8)
        for copy in copies(t):
            copy.wait()
        for c in range(line // LANES):
            cols = slice(c * LANES, (c + 1) * LANES)
            reverse = o_ref[at, cols] == 1
            passed, colors = [], []
            for k in range(depth):
                *color, extinction = look_up(table, b[k, at, cols])
                passed.append(jnp.exp2(extinction * scale * d_ref[k, inner, cols]))
                colors.append(color)
            t0, t1, t2, t3 = passed
            front, back = t0 * t1, t2 * t3
            ahead = [
                jnp.where(reverse, t1 * back, 1.0),
                jnp.where(reverse, back, t0),
                jnp.where(reverse, t3, front),
                jnp.where(reverse, 1.0, front * t2),
            ]
            for k in range(depth):
                weight = (1.0 - passed[k]) * (1.0 / UNIT) * ahead[k]
                for i in range(3):
                    w_ref[k, i, at, cols] = colors[k][i] * weight
            l_ref[at, cols] = front * back
        return carry

    lax.fori_loop(0, rows // 8, tile, 0)


def look(density, bins, order, table, spacing):
    depth, rows, line = density.shape
    vmem = pl.BlockSpec(memory_space=pltpu.VMEM)
    hbm = pl.BlockSpec(memory_space=pl.ANY)
    cells = depth * rows * line
    return pl.pallas_call(
        lambda *refs: look_kernel(spacing, *refs),
        out_shape=[
            jax.ShapeDtypeStruct((depth, rows + 16, line), F32),
            jax.ShapeDtypeStruct((depth, 3, rows, line), F32),
            jax.ShapeDtypeStruct((rows, line), F32),
            jax.ShapeDtypeStruct((rows, line), jnp.int32),
        ],
        in_specs=[hbm] * 3 + [vmem],
        out_specs=[vmem] * 4,
        scratch_shapes=[
            pltpu.VMEM((depth, rows, line), jnp.int32),
            pltpu.SemaphoreType.DMA((3, rows // 8)),
        ],
        compiler_params=params(12),
        cost_estimate=pl.CostEstimate(
            flops=50 * cells, bytes_accessed=12 * cells, transcendentals=cells
        ),
        name="look",
    )(density, bins, order, table)


def slopes_kernel(d_in, w_ref, ya_ref, yb_ref, d, c_ref, a_ref, n_ref):
    depth, rows, line = d.shape[0], d.shape[1] - 16, d.shape[2]
    chunks = line // LANES
    lat = lax.axis_index("lat")
    lat_odd = (lat & 1) == 1
    keep_low = jnp.where(lat == 0, 0.0, 1.0).astype(F32)
    keep_high = jnp.where(lat == lax.axis_size("lat") - 1, 0.0, 1.0).astype(F32)
    for k in range(depth):
        from_a, from_b = ya_ref[k : k + 1, :], yb_ref[k : k + 1, :]
        d[k, 7:8, :] = jnp.where(lat_odd, from_a, from_b) * keep_low
        d[k, rows + 8 : rows + 9, :] = jnp.where(lat_odd, from_b, from_a) * keep_high
    lane = lax.broadcasted_iota(jnp.int32, (8, LANES), 1)
    sub = lax.broadcasted_iota(jnp.int32, (8, LANES), 0)
    first_lane, last_lane = lane == 0, lane == LANES - 1
    first_sub, last_sub = sub == 0, sub == 7

    def tile(t, carry):
        base = pl.multiple_of(t * 8, 8)
        at = pl.ds(base, 8)
        for c in range(chunks):
            cols = slice(c * LANES, (c + 1) * LANES)

            def cell(k, row, column=c):
                return d[k, pl.ds(row, 8), column * LANES : (column + 1) * LANES]

            total = [None, None, None]
            for k in range(depth):
                here = cell(k, base + 8)
                before, after = cell(k, base), cell(k, base + 16)
                left = cell(k, base + 8, c - 1) if c > 0 else jnp.zeros_like(here)
                right = cell(k, base + 8, c + 1) if c < chunks - 1 else jnp.zeros_like(here)
                step_x = pltpu.roll(jnp.where(first_lane, right, here), LANES - 1, 1) - pltpu.roll(
                    jnp.where(last_lane, left, here), 1, 1
                )
                step_y = pltpu.roll(jnp.where(first_sub, after, here), 7, 0) - pltpu.roll(
                    jnp.where(last_sub, before, here), 1, 0
                )
                tilt = LIGHT_X * step_x + LIGHT_Y * step_y
                norm = step_x * step_x + step_y * step_y + 1.0
                if k in (0, depth - 1):
                    a_ref[min(k, 1), at, cols] = tilt
                    n_ref[min(k, 1), at, cols] = norm
                    continue
                step_z = cell(k + 1, base + 8) - cell(k - 1, base + 8)
                shade = 1.0 + (tilt + LIGHT_Z * step_z) * lax.rsqrt(norm + step_z * step_z)
                for i in range(3):
                    term = w_ref[k, i, at, cols] * shade
                    total[i] = term if total[i] is None else total[i] + term
            for i in range(3):
                c_ref[i, at, cols] = total[i]
        return carry

    lax.fori_loop(0, rows // 8, tile, 0)


def slopes(density, weight, ya, yb):
    depth, rows, line = density.shape
    rows -= 16
    vmem = pl.BlockSpec(memory_space=pltpu.VMEM)
    cells = depth * rows * line
    return pl.pallas_call(
        slopes_kernel,
        out_shape=[
            jax.ShapeDtypeStruct(density.shape, F32),
            jax.ShapeDtypeStruct((3, rows, line), F32),
            jax.ShapeDtypeStruct((2, rows, line), F32),
            jax.ShapeDtypeStruct((2, rows, line), F32),
        ],
        in_specs=[vmem] * 4,
        out_specs=[vmem] * 4,
        input_output_aliases={0: 0},
        compiler_params=params(12),
        cost_estimate=pl.CostEstimate(
            flops=50 * cells, bytes_accessed=12 * cells, transcendentals=cells
        ),
        name="slopes",
    )(density, weight, ya, yb)


def swap_pieces(tiles, sub):
    for size in (4, 2):
        keep = (sub & size) == 0
        step = size // 2
        result = list(tiles)
        for i in range(4):
            if i & step == 0:
                a, b = tiles[i], tiles[i | step]
                result[i] = jnp.where(keep, a, pltpu.roll(b, size, 0))
                result[i | step] = jnp.where(keep, pltpu.roll(a, 8 - size, 0), b)
        tiles = result
    return tiles


def edges_kernel(d_ref, za_ref, zb_ref, o_ref, c_ref, w_ref, l_ref, a_ref, n_ref, *rest):
    outs, mask_ref, s = rest[:8], rest[8], rest[9]
    depth, line = d_ref.shape[0], d_ref.shape[2]
    slab = lax.axis_index("slab")
    slab_odd = (slab & 1) == 1
    keep_low = jnp.where(slab == 0, 0.0, 1.0).astype(F32)
    keep_high = jnp.where(slab == lax.axis_size("slab") - 1, 0.0, 1.0).astype(F32)
    sub = lax.broadcasted_iota(jnp.int32, (8, LANES), 0)
    chunks = line // LANES

    def part(index, carry):
        half, c = index // chunks, index % chunks
        cols = pl.ds(pl.multiple_of(c * LANES, LANES), LANES)
        channels = [[] for _ in range(5)]
        for quarter in range(4):
            at = pl.ds(pl.multiple_of(16 * quarter + 8 * half, 8), 8)
            inner = pl.ds(pl.multiple_of(16 * quarter + 8 * half + 8, 8), 8)
            from_a, from_b = za_ref[at, cols], zb_ref[at, cols]
            below = jnp.where(slab_odd, from_a, from_b) * keep_low
            above = jnp.where(slab_odd, from_b, from_a) * keep_high
            total = [c_ref[i, at, cols] for i in range(3)]
            steps = (d_ref[1, inner, cols] - below, above - d_ref[depth - 2, inner, cols])
            for edge in range(2):
                step_z = steps[edge]
                shade = 1.0 + (a_ref[edge, at, cols] + LIGHT_Z * step_z) * lax.rsqrt(
                    n_ref[edge, at, cols] + step_z * step_z
                )
                for i in range(3):
                    total[i] = total[i] + w_ref[edge * (depth - 1), i, at, cols] * shade
            for i in range(3):
                channels[i].append(total[i])
            channels[3].append(l_ref[at, cols])
            channels[4].append(o_ref[at, cols].astype(F32))
        for i in range(5):
            for piece, value in enumerate(swap_pieces(channels[i], sub)):
                s[4 * half + piece, i, :, cols] = value
        return carry

    lax.fori_loop(0, 2 * chunks, part, 0)
    place = slab & 7
    for j in range(8):
        for i in range(4):
            outs[j][i] = s[place ^ j, i]
    mask_ref[...] = s[place, 4]


def edges(density, za, zb, order, color, weight, light, tilt, norm):
    depth, rows, line = density.shape
    rows -= 16
    vmem = pl.BlockSpec(memory_space=pltpu.VMEM)
    return pl.pallas_call(
        edges_kernel,
        out_shape=[jax.ShapeDtypeStruct((4, 8, line), F32)] * 8
        + [jax.ShapeDtypeStruct((8, line), F32)],
        in_specs=[vmem] * 9,
        out_specs=[vmem] * 9,
        scratch_shapes=[pltpu.VMEM((8, 5, 8, line), F32)],
        compiler_params=params(12),
        cost_estimate=pl.CostEstimate(
            flops=40 * depth * rows * line, bytes_accessed=4 * depth * rows * line, transcendentals=depth * rows * line
        ),
        name="edges",
    )(density, za, zb, order, color, weight, light, tilt, norm)


def merge(a, b, b_first):
    front = [jnp.where(b_first, y, x) for x, y in zip(a, b)]
    back = [jnp.where(b_first, x, y) for x, y in zip(a, b)]
    return [front[i] + front[3] * back[i] for i in range(3)] + [front[3] * back[3]]


def merge_tree(blocks, mask, place):
    bit = 0
    while len(blocks) > 1:
        b_first = jnp.logical_xor(mask > 0.5, (place >> bit & 1) == 1)
        blocks = [merge(blocks[i], blocks[i + 1], b_first) for i in range(0, len(blocks), 2)]
        bit += 1
    return blocks[0]


def eight_kernel(*refs):
    ins, mask_ref, outs, own_mask = refs[:8], refs[8], refs[9:13], refs[13]
    line = mask_ref.shape[1]
    slab = lax.axis_index("slab")
    place, quarter = slab & 7, slab >> 3
    sub = lax.broadcasted_iota(jnp.int32, (8, LANES), 0) // 2

    def part(c, carry):
        cols = pl.ds(pl.multiple_of(c * LANES, LANES), LANES)
        mask = mask_ref[:, cols]
        blocks = [[ins[ORDER8.index(j)][i, :, cols] for i in range(4)] for j in range(8)]
        merged = merge_tree(blocks, mask, place)
        for j in range(4):
            target = quarter ^ j
            packed = None
            for i in range(4):
                moved = pltpu.roll(merged[i], (2 * i + 8 - 2 * target) & 7, 0)
                packed = moved if packed is None else jnp.where(sub == i, moved, packed)
            outs[j][:, cols] = packed
        own_mask[:, cols] = pltpu.roll(mask, (8 - 2 * quarter) & 7, 0)
        return carry

    lax.fori_loop(0, line // LANES, part, 0)


def merge_eight(blocks, mask):
    line = mask.shape[1]
    vmem = pl.BlockSpec(memory_space=pltpu.VMEM)
    return pl.pallas_call(
        eight_kernel,
        out_shape=[jax.ShapeDtypeStruct((8, line), F32)] * 5,
        in_specs=[vmem] * 9,
        out_specs=[vmem] * 5,
        compiler_params=params(6),
        name="merge_eight",
    )(*[blocks[j] for j in ORDER8], mask)


def four_kernel(*refs):
    ins, mask_ref, out = refs[:4], refs[4], refs[5]
    place = lax.axis_index("slab") >> 3
    mask = mask_ref[0:2, :]
    blocks = [[ins[ORDER4.index(j)][2 * i : 2 * i + 2, :] for i in range(4)] for j in range(4)]
    merged = merge_tree(blocks, mask, place)
    for i in range(3):
        out[i] = merged[i]
    out[3] = 1.0 - merged[3]


def merge_four(blocks, mask):
    line = mask.shape[1]
    vmem = pl.BlockSpec(memory_space=pltpu.VMEM)
    return pl.pallas_call(
        four_kernel,
        out_shape=jax.ShapeDtypeStruct((4, 2, line), F32),
        in_specs=[vmem] * 5,
        out_specs=vmem,
        compiler_params=params(4),
        name="merge_four",
    )(*[blocks[j] for j in ORDER4], mask)


def swap(block, axis, step):
    count = lax.axis_size(axis)
    return lax.ppermute(block, axis, [(i, i ^ step) for i in range(count)])


def swap_odd(block, axis):
    count = lax.axis_size(axis)
    route = []
    for i in range(1, count, 2):
        route += [(i, (i + 1) % count), ((i + 1) % count, i)]
    return lax.ppermute(block, axis, route)


def shards(density, bins, transfer, depth_order):
    depth_cells = density.shape[0]
    spacing = 1.5 / (depth_cells * lax.axis_size("slab"))
    density, bins, transfer, depth_order = (
        pltpu.with_memory_space_constraint(x, pltpu.HBM)
        for x in (density, bins, transfer, depth_order)
    )
    za, zb, ya, yb, table = faces(density, transfer)
    za, zb = swap(za, "slab", 1), swap_odd(zb, "slab")
    ya, yb = swap(ya, "lat", 1), swap_odd(yb, "lat")
    density, weight, light, order = look(density, bins, depth_order, table, spacing)
    density, color, tilt, norm = slopes(density, weight, ya, yb)
    *blocks, mask = edges(density, za, zb, order, color, weight, light, tilt, norm)
    blocks = blocks[:1] + [swap(blocks[j], "slab", j) for j in range(1, 8)]
    *quarters, mask = merge_eight(blocks, mask)
    quarters = quarters[:1] + [swap(quarters[j], "slab", 8 * j) for j in range(1, 4)]
    return merge_four(quarters, mask)


def solution(mesh):
    return jax.shard_map(
        shards,
        mesh=mesh,
        in_specs=(P("slab", "lat", None), P("slab", "lat", None), P(), P("lat", None)),
        out_specs=P(None, ("lat", "slab"), None),
        check_vma=False,
    )
```

```python
import math

import jax
import jax.numpy as jnp
from jax import lax
from jax.experimental import pallas as pl
from jax.experimental.pallas import tpu as pltpu
from jax.sharding import PartitionSpec as P

LIGHT_X = 0.48
LIGHT_Y = 0.6
LIGHT_Z = 0.64
UNIT = 2048.0
LANES = 128
MIB = 1024 * 1024
F32 = jnp.float32
ORDER8 = (1, 7, 6, 5, 3, 4, 2, 0)
ORDER4 = (2, 3, 1, 0)


def params(mib):
    return pltpu.CompilerParams(vmem_limit_bytes=mib * MIB)


def faces_kernel(d_ref, t_ref, za_ref, zb_ref, ya_ref, yb_ref, table_ref, low, high, t, sems):
    depth, rows = d_ref.shape[0], d_ref.shape[1]
    slab_odd = lax.axis_index("slab") & 1
    lat_odd = lax.axis_index("lat") & 1
    last = depth - 1
    copies = [
        pltpu.make_async_copy(d_ref.at[last - last * slab_odd], za_ref, sems.at[0]),
        pltpu.make_async_copy(d_ref.at[last * slab_odd], zb_ref, sems.at[1]),
        pltpu.make_async_copy(d_ref.at[:, pl.ds(0, 8)], low, sems.at[2]),
        pltpu.make_async_copy(d_ref.at[:, pl.ds(rows - 8, 8)], high, sems.at[3]),
        pltpu.make_async_copy(t_ref, t, sems.at[4]),
    ]
    for copy in copies:
        copy.start()
    copies[4].wait()
    units = (t[...].astype(F32) * UNIT).astype(jnp.int32)
    red, green, blue, extinction = (units[i : i + 1] for i in range(4))
    word = red | (green << 12) | (blue << 24)
    rest = extinction | ((blue >> 8) << 12)
    halves = slice(0, LANES), slice(LANES, 2 * LANES)
    parts = [word[:, half] for half in halves] + [rest[:, halves[0]] | (rest[:, halves[1]] << 16)]
    for i, part in enumerate(parts):
        table_ref[i] = jnp.broadcast_to(part, (8, LANES))
    copies[2].wait()
    copies[3].wait()
    odd = lat_odd == 1
    for k in range(depth):
        first, final = low[k, 0:1], high[k, 7:8]
        ya_ref[k : k + 1, :] = jnp.where(odd, first, final)
        yb_ref[k : k + 1, :] = jnp.where(odd, final, first)
    copies[0].wait()
    copies[1].wait()


def faces(density, transfer):
    depth, rows, line = density.shape
    return pl.pallas_call(
        faces_kernel,
        out_shape=[
            jax.ShapeDtypeStruct((rows, line), F32),
            jax.ShapeDtypeStruct((rows, line), F32),
            jax.ShapeDtypeStruct((depth, line), F32),
            jax.ShapeDtypeStruct((depth, line), F32),
            jax.ShapeDtypeStruct((3, 8, LANES), jnp.int32),
        ],
        in_specs=[pl.BlockSpec(memory_space=pl.ANY)] * 2,
        out_specs=[pl.BlockSpec(memory_space=pl.ANY)] * 2
        + [pl.BlockSpec(memory_space=pltpu.VMEM)] * 3,
        scratch_shapes=[
            pltpu.VMEM((depth, 8, line), F32),
            pltpu.VMEM((depth, 8, line), F32),
            pltpu.VMEM(transfer.shape, transfer.dtype),
            pltpu.SemaphoreType.DMA((5,)),
        ],
        compiler_params=params(4),
        name="faces",
    )(density, transfer)


def columns_of(table, column):
    numbers = lax.GatherDimensionNumbers(
        offset_dims=(),
        collapsed_slice_dims=(1,),
        start_index_map=(1,),
        operand_batching_dims=(0,),
        start_indices_batching_dims=(0,),
    )
    return lax.gather(
        table, column[..., None], numbers, (1, 1), mode=lax.GatherScatterMode.PROMISE_IN_BOUNDS
    )


def look_up(table, bins):
    column = bins & (LANES - 1)
    upper = bins >= LANES
    low_half, high_half, rest = (columns_of(part, column) for part in table)
    word = jnp.where(upper, high_half, low_half)
    rest = jnp.where(upper, rest >> 16, rest)
    blue = ((rest >> 4) & 0xF00) | lax.shift_right_logical(word, 24)
    units = (word & 0xFFF, (word >> 12) & 0xFFF, blue, rest & 0xFFF)
    return [value.astype(F32) for value in units]


def look_kernel(spacing, d_hbm, b_hbm, o_hbm, t_ref, d_ref, w_ref, l_ref, o_ref, b, sems):
    depth, rows, line = d_hbm.shape

    cuts = (0, 8, 32, rows)

    def copies(part):
        first, size = cuts[part], cuts[part + 1] - cuts[part]
        at, inner = pl.ds(first, size), pl.ds(first + 8, size)
        return [
            pltpu.make_async_copy(b_hbm.at[:, at], b.at[:, at], sems.at[0, part]),
            pltpu.make_async_copy(d_hbm.at[:, at], d_ref.at[:, inner], sems.at[1, part]),
            pltpu.make_async_copy(o_hbm.at[at], o_ref.at[at], sems.at[2, part]),
        ]

    for part in range(len(cuts) - 1):
        for copy in copies(part):
            copy.start()
    table = [t_ref[i] for i in range(3)]
    scale = -spacing / (UNIT * math.log(2.0))

    def tile(t, carry):
        at = pl.ds(pl.multiple_of(t * 8, 8), 8)
        inner = pl.ds(pl.multiple_of(t * 8 + 8, 8), 8)
        for part in range(len(cuts) - 1):

            @pl.when(t * 8 == cuts[part])
            def _(part=part):
                for copy in copies(part):
                    copy.wait()

        for c in range(line // LANES):
            cols = slice(c * LANES, (c + 1) * LANES)
            reverse = o_ref[at, cols] == 1
            passed, colors = [], []
            for k in range(depth):
                *color, extinction = look_up(table, b[k, at, cols])
                passed.append(jnp.exp2(extinction * scale * d_ref[k, inner, cols]))
                colors.append(color)
            t0, t1, t2, t3 = passed
            front, back = t0 * t1, t2 * t3
            ahead = [
                jnp.where(reverse, t1 * back, 1.0),
                jnp.where(reverse, back, t0),
                jnp.where(reverse, t3, front),
                jnp.where(reverse, 1.0, front * t2),
            ]
            for k in range(depth):
                weight = (1.0 - passed[k]) * (1.0 / UNIT) * ahead[k]
                for i in range(3):
                    w_ref[k, i, at, cols] = colors[k][i] * weight
            l_ref[at, cols] = front * back
        return carry

    lax.fori_loop(0, rows // 8, tile, 0)


def look(density, bins, order, table, spacing):
    depth, rows, line = density.shape
    vmem = pl.BlockSpec(memory_space=pltpu.VMEM)
    hbm = pl.BlockSpec(memory_space=pl.ANY)
    cells = depth * rows * line
    return pl.pallas_call(
        lambda *refs: look_kernel(spacing, *refs),
        out_shape=[
            jax.ShapeDtypeStruct((depth, rows + 16, line), F32),
            jax.ShapeDtypeStruct((depth, 3, rows, line), F32),
            jax.ShapeDtypeStruct((rows, line), F32),
            jax.ShapeDtypeStruct((rows, line), jnp.int32),
        ],
        in_specs=[hbm] * 3 + [vmem],
        out_specs=[vmem] * 4,
        scratch_shapes=[
            pltpu.VMEM((depth, rows, line), jnp.int32),
            pltpu.SemaphoreType.DMA((3, 3)),
        ],
        compiler_params=params(12),
        cost_estimate=pl.CostEstimate(
            flops=50 * cells, bytes_accessed=12 * cells, transcendentals=cells
        ),
        name="look",
    )(density, bins, order, table)


def slopes_kernel(d_in, w_ref, ya_ref, yb_ref, d, c_ref, a_ref, n_ref):
    depth, rows, line = d.shape[0], d.shape[1] - 16, d.shape[2]
    chunks = line // LANES
    lat = lax.axis_index("lat")
    lat_odd = (lat & 1) == 1
    keep_low = jnp.where(lat == 0, 0.0, 1.0).astype(F32)
    keep_high = jnp.where(lat == lax.axis_size("lat") - 1, 0.0, 1.0).astype(F32)
    for k in range(depth):
        from_a, from_b = ya_ref[k : k + 1, :], yb_ref[k : k + 1, :]
        d[k, 7:8, :] = jnp.where(lat_odd, from_a, from_b) * keep_low
        d[k, rows + 8 : rows + 9, :] = jnp.where(lat_odd, from_b, from_a) * keep_high
    lane = lax.broadcasted_iota(jnp.int32, (8, LANES), 1)
    sub = lax.broadcasted_iota(jnp.int32, (8, LANES), 0)
    first_lane, last_lane = lane == 0, lane == LANES - 1
    first_sub, last_sub = sub == 0, sub == 7

    def tile(t, carry):
        base = pl.multiple_of(t * 8, 8)
        at = pl.ds(base, 8)
        for c in range(chunks):
            cols = slice(c * LANES, (c + 1) * LANES)

            def cell(k, row, column=c):
                return d[k, pl.ds(row, 8), column * LANES : (column + 1) * LANES]

            total = [None, None, None]
            for k in range(depth):
                here = cell(k, base + 8)
                before, after = cell(k, base), cell(k, base + 16)
                left = cell(k, base + 8, c - 1) if c > 0 else jnp.zeros_like(here)
                right = cell(k, base + 8, c + 1) if c < chunks - 1 else jnp.zeros_like(here)
                step_x = pltpu.roll(jnp.where(first_lane, right, here), LANES - 1, 1) - pltpu.roll(
                    jnp.where(last_lane, left, here), 1, 1
                )
                step_y = pltpu.roll(jnp.where(first_sub, after, here), 7, 0) - pltpu.roll(
                    jnp.where(last_sub, before, here), 1, 0
                )
                tilt = LIGHT_X * step_x + LIGHT_Y * step_y
                norm = step_x * step_x + step_y * step_y + 1.0
                if k in (0, depth - 1):
                    a_ref[min(k, 1), at, cols] = tilt
                    n_ref[min(k, 1), at, cols] = norm
                    continue
                step_z = cell(k + 1, base + 8) - cell(k - 1, base + 8)
                shade = 1.0 + (tilt + LIGHT_Z * step_z) * lax.rsqrt(norm + step_z * step_z)
                for i in range(3):
                    term = w_ref[k, i, at, cols] * shade
                    total[i] = term if total[i] is None else total[i] + term
            for i in range(3):
                c_ref[i, at, cols] = total[i]
        return carry

    lax.fori_loop(0, rows // 8, tile, 0)


def slopes(density, weight, ya, yb):
    depth, rows, line = density.shape
    rows -= 16
    vmem = pl.BlockSpec(memory_space=pltpu.VMEM)
    cells = depth * rows * line
    return pl.pallas_call(
        slopes_kernel,
        out_shape=[
            jax.ShapeDtypeStruct(density.shape, F32),
            jax.ShapeDtypeStruct((3, rows, line), F32),
            jax.ShapeDtypeStruct((2, rows, line), F32),
            jax.ShapeDtypeStruct((2, rows, line), F32),
        ],
        in_specs=[vmem] * 4,
        out_specs=[vmem] * 4,
        input_output_aliases={0: 0},
        compiler_params=params(12),
        cost_estimate=pl.CostEstimate(
            flops=50 * cells, bytes_accessed=12 * cells, transcendentals=cells
        ),
        name="slopes",
    )(density, weight, ya, yb)


def swap_pieces(tiles, sub):
    for size in (4, 2):
        keep = (sub & size) == 0
        step = size // 2
        result = list(tiles)
        for i in range(4):
            if i & step == 0:
                a, b = tiles[i], tiles[i | step]
                result[i] = jnp.where(keep, a, pltpu.roll(b, size, 0))
                result[i | step] = jnp.where(keep, pltpu.roll(a, 8 - size, 0), b)
        tiles = result
    return tiles


def edges_kernel(d_ref, zb_ref, za_ref, o_ref, c_ref, w_ref, l_ref, a_ref, n_ref, *rest):
    outs, mask_ref, s = rest[:8], rest[8], rest[9]
    depth, line = d_ref.shape[0], d_ref.shape[2]
    slab = lax.axis_index("slab")
    slab_odd = (slab & 1) == 1
    keep_low = jnp.where(slab == 0, 0.0, 1.0).astype(F32)
    keep_high = jnp.where(slab == lax.axis_size("slab") - 1, 0.0, 1.0).astype(F32)
    sub = lax.broadcasted_iota(jnp.int32, (8, LANES), 0)
    chunks = line // LANES

    def part(index, carry):
        half, c = index // chunks, index % chunks
        cols = pl.ds(pl.multiple_of(c * LANES, LANES), LANES)
        channels = [[] for _ in range(5)]
        for quarter in range(4):
            at = pl.ds(pl.multiple_of(16 * quarter + 8 * half, 8), 8)
            inner = pl.ds(pl.multiple_of(16 * quarter + 8 * half + 8, 8), 8)
            from_a, from_b = za_ref[at, cols], zb_ref[at, cols]
            below = jnp.where(slab_odd, from_a, from_b) * keep_low
            above = jnp.where(slab_odd, from_b, from_a) * keep_high
            total = [c_ref[i, at, cols] for i in range(3)]
            steps = (d_ref[1, inner, cols] - below, above - d_ref[depth - 2, inner, cols])
            for edge in range(2):
                step_z = steps[edge]
                shade = 1.0 + (a_ref[edge, at, cols] + LIGHT_Z * step_z) * lax.rsqrt(
                    n_ref[edge, at, cols] + step_z * step_z
                )
                for i in range(3):
                    total[i] = total[i] + w_ref[edge * (depth - 1), i, at, cols] * shade
            for i in range(3):
                channels[i].append(total[i])
            channels[3].append(l_ref[at, cols])
            channels[4].append(o_ref[at, cols].astype(F32))
        for i in range(5):
            for piece, value in enumerate(swap_pieces(channels[i], sub)):
                s[4 * half + piece, i, :, cols] = value
        return carry

    lax.fori_loop(0, 2 * chunks, part, 0)
    place = slab & 7
    for j in range(8):
        for i in range(4):
            outs[j][i] = s[place ^ j, i]
    mask_ref[...] = s[place, 4]


def edges(density, za, zb, order, color, weight, light, tilt, norm):
    depth, rows, line = density.shape
    rows -= 16
    vmem = pl.BlockSpec(memory_space=pltpu.VMEM)
    return pl.pallas_call(
        edges_kernel,
        out_shape=[jax.ShapeDtypeStruct((4, 8, line), F32)] * 8
        + [jax.ShapeDtypeStruct((8, line), F32)],
        in_specs=[vmem] * 9,
        out_specs=[vmem] * 9,
        scratch_shapes=[pltpu.VMEM((8, 5, 8, line), F32)],
        compiler_params=params(12),
        cost_estimate=pl.CostEstimate(
            flops=40 * depth * rows * line, bytes_accessed=4 * depth * rows * line, transcendentals=depth * rows * line
        ),
        name="edges",
    )(density, zb, za, order, color, weight, light, tilt, norm)


def merge(a, b, b_first):
    front = [jnp.where(b_first, y, x) for x, y in zip(a, b)]
    back = [jnp.where(b_first, x, y) for x, y in zip(a, b)]
    return [front[i] + front[3] * back[i] for i in range(3)] + [front[3] * back[3]]


def merge_tree(blocks, mask, place):
    bit = 0
    while len(blocks) > 1:
        b_first = jnp.logical_xor(mask > 0.5, (place >> bit & 1) == 1)
        blocks = [merge(blocks[i], blocks[i + 1], b_first) for i in range(0, len(blocks), 2)]
        bit += 1
    return blocks[0]


def eight_kernel(*refs):
    ins, mask_ref, outs, own_mask = refs[:8], refs[8], refs[9:13], refs[13]
    line = mask_ref.shape[1]
    slab = lax.axis_index("slab")
    place, quarter = slab & 7, slab >> 3
    sub = lax.broadcasted_iota(jnp.int32, (8, LANES), 0) // 2

    def part(c, carry):
        cols = pl.ds(pl.multiple_of(c * LANES, LANES), LANES)
        mask = mask_ref[:, cols]
        blocks = [[ins[ORDER8.index(j)][i, :, cols] for i in range(4)] for j in range(8)]
        merged = merge_tree(blocks, mask, place)
        for j in range(4):
            target = quarter ^ j
            packed = None
            for i in range(4):
                moved = pltpu.roll(merged[i], (2 * i + 8 - 2 * target) & 7, 0)
                packed = moved if packed is None else jnp.where(sub == i, moved, packed)
            outs[j][:, cols] = packed
        own_mask[:, cols] = pltpu.roll(mask, (8 - 2 * quarter) & 7, 0)
        return carry

    lax.fori_loop(0, line // LANES, part, 0)


def merge_eight(blocks, mask):
    line = mask.shape[1]
    vmem = pl.BlockSpec(memory_space=pltpu.VMEM)
    return pl.pallas_call(
        eight_kernel,
        out_shape=[jax.ShapeDtypeStruct((8, line), F32)] * 5,
        in_specs=[vmem] * 9,
        out_specs=[vmem] * 5,
        compiler_params=params(6),
        name="merge_eight",
    )(*[blocks[j] for j in ORDER8], mask)


def four_kernel(*refs):
    ins, mask_ref, out = refs[:4], refs[4], refs[5]
    place = lax.axis_index("slab") >> 3
    mask = mask_ref[0:2, :]
    blocks = [[ins[ORDER4.index(j)][2 * i : 2 * i + 2, :] for i in range(4)] for j in range(4)]
    merged = merge_tree(blocks, mask, place)
    for i in range(3):
        out[i] = merged[i]
    out[3] = 1.0 - merged[3]


def merge_four(blocks, mask):
    line = mask.shape[1]
    vmem = pl.BlockSpec(memory_space=pltpu.VMEM)
    return pl.pallas_call(
        four_kernel,
        out_shape=jax.ShapeDtypeStruct((4, 2, line), F32),
        in_specs=[vmem] * 5,
        out_specs=vmem,
        compiler_params=params(4),
        name="merge_four",
    )(*[blocks[j] for j in ORDER4], mask)


def swap(block, axis, step):
    count = lax.axis_size(axis)
    return lax.ppermute(block, axis, [(i, i ^ step) for i in range(count)])


def swap_odd(block, axis):
    slabs, lats = lax.axis_size("slab"), lax.axis_size("lat")
    route = []
    for slab in range(slabs):
        for lat in range(lats):
            at, count = (slab, slabs) if axis == "slab" else (lat, lats)
            step = 2 * (at & 1) - 1
            if at in (0, count - 1):
                partner = (slab, lat ^ 1) if axis == "slab" else (slab ^ 1, lat)
            else:
                partner = (slab + step, lat) if axis == "slab" else (slab, lat + step)
            route.append((slab * lats + lat, partner[0] * lats + partner[1]))
    return lax.ppermute(block, ("slab", "lat"), route)


def shards(density, bins, transfer, depth_order):
    depth_cells = density.shape[0]
    spacing = 1.5 / (depth_cells * lax.axis_size("slab"))
    density, bins, transfer, depth_order = (
        pltpu.with_memory_space_constraint(x, pltpu.HBM)
        for x in (density, bins, transfer, depth_order)
    )
    za, zb, ya, yb, table = faces(density, transfer)
    za, zb = swap(za, "slab", 1), swap_odd(zb, "slab")
    ya, yb = swap(ya, "lat", 1), swap_odd(yb, "lat")
    density, weight, light, order = look(density, bins, depth_order, table, spacing)
    density, color, tilt, norm = slopes(density, weight, ya, yb)
    *blocks, mask = edges(density, za, zb, order, color, weight, light, tilt, norm)
    blocks = blocks[:1] + [swap(blocks[j], "slab", j) for j in range(1, 8)]
    *quarters, mask = merge_eight(blocks, mask)
    quarters = quarters[:1] + [swap(quarters[j], "slab", 8 * j) for j in range(1, 4)]
    return merge_four(quarters, mask)


def solution(mesh):
    return jax.shard_map(
        shards,
        mesh=mesh,
        in_specs=(P("slab", "lat", None), P("slab", "lat", None), P(), P("lat", None)),
        out_specs=P(None, ("lat", "slab"), None),
        check_vma=False,
    )
```

```python
import math

import jax
import jax.numpy as jnp
from jax import lax
from jax.experimental import pallas as pl
from jax.experimental.pallas import tpu as pltpu
from jax.sharding import PartitionSpec as P

LIGHT_X = 0.48
LIGHT_Y = 0.6
LIGHT_Z = 0.64
UNIT = 2048.0
LANES = 128
MIB = 1024 * 1024
F32 = jnp.float32
ORDER8 = (1, 7, 3, 5, 2, 6, 4, 0)
ORDER4 = (2, 3, 1, 0)


def params(mib):
    return pltpu.CompilerParams(vmem_limit_bytes=mib * MIB)


def faces_kernel(d_ref, t_ref, za_ref, zb_ref, ya_ref, yb_ref, table_ref, low, high, t, sems):
    depth, rows = d_ref.shape[0], d_ref.shape[1]
    slab_odd = lax.axis_index("slab") & 1
    lat_odd = lax.axis_index("lat") & 1
    last = depth - 1
    copies = [
        pltpu.make_async_copy(d_ref.at[last - last * slab_odd], za_ref, sems.at[0]),
        pltpu.make_async_copy(d_ref.at[last * slab_odd], zb_ref, sems.at[1]),
        pltpu.make_async_copy(d_ref.at[:, pl.ds(0, 8)], low, sems.at[2]),
        pltpu.make_async_copy(d_ref.at[:, pl.ds(rows - 8, 8)], high, sems.at[3]),
        pltpu.make_async_copy(t_ref, t, sems.at[4]),
    ]
    for copy in copies:
        copy.start()
    copies[4].wait()
    units = (t[...].astype(F32) * UNIT).astype(jnp.int32)
    red, green, blue, extinction = (units[i : i + 1] for i in range(4))
    word = red | (green << 12) | (blue << 24)
    rest = extinction | ((blue >> 8) << 12)
    halves = slice(0, LANES), slice(LANES, 2 * LANES)
    parts = [word[:, half] for half in halves] + [rest[:, halves[0]] | (rest[:, halves[1]] << 16)]
    for i, part in enumerate(parts):
        table_ref[i] = jnp.broadcast_to(part, (8, LANES))
    copies[2].wait()
    copies[3].wait()
    odd = lat_odd == 1
    for k in range(depth):
        first, final = low[k, 0:1], high[k, 7:8]
        ya_ref[k : k + 1, :] = jnp.where(odd, first, final)
        yb_ref[k : k + 1, :] = jnp.where(odd, final, first)
    copies[0].wait()
    copies[1].wait()


def faces(density, transfer):
    depth, rows, line = density.shape
    return pl.pallas_call(
        faces_kernel,
        out_shape=[
            jax.ShapeDtypeStruct((rows, line), F32),
            jax.ShapeDtypeStruct((rows, line), F32),
            jax.ShapeDtypeStruct((depth, line), F32),
            jax.ShapeDtypeStruct((depth, line), F32),
            jax.ShapeDtypeStruct((3, 8, LANES), jnp.int32),
        ],
        in_specs=[pl.BlockSpec(memory_space=pl.ANY)] * 2,
        out_specs=[pl.BlockSpec(memory_space=pl.ANY)] * 2
        + [pl.BlockSpec(memory_space=pltpu.VMEM)] * 3,
        scratch_shapes=[
            pltpu.VMEM((depth, 8, line), F32),
            pltpu.VMEM((depth, 8, line), F32),
            pltpu.VMEM(transfer.shape, transfer.dtype),
            pltpu.SemaphoreType.DMA((5,)),
        ],
        compiler_params=params(4),
        name="faces",
    )(density, transfer)


def columns_of(table, column):
    numbers = lax.GatherDimensionNumbers(
        offset_dims=(),
        collapsed_slice_dims=(1,),
        start_index_map=(1,),
        operand_batching_dims=(0,),
        start_indices_batching_dims=(0,),
    )
    return lax.gather(
        table, column[..., None], numbers, (1, 1), mode=lax.GatherScatterMode.PROMISE_IN_BOUNDS
    )


def look_up(table, bins):
    column = bins & (LANES - 1)
    upper = bins >= LANES
    low_half, high_half, rest = (columns_of(part, column) for part in table)
    word = jnp.where(upper, high_half, low_half)
    rest = jnp.where(upper, rest >> 16, rest)
    blue = ((rest >> 4) & 0xF00) | lax.shift_right_logical(word, 24)
    units = (word & 0xFFF, (word >> 12) & 0xFFF, blue, rest & 0xFFF)
    return [value.astype(F32) for value in units]


def look_kernel(spacing, d_hbm, b_hbm, o_hbm, t_ref, d_ref, w_ref, l_ref, o_ref, b, sems):
    depth, rows, line = d_hbm.shape

    cuts = (0, 8, 32, rows)

    def copies(part):
        first, size = cuts[part], cuts[part + 1] - cuts[part]
        at, inner = pl.ds(first, size), pl.ds(first + 8, size)
        return [
            pltpu.make_async_copy(b_hbm.at[:, at], b.at[:, at], sems.at[0, part]),
            pltpu.make_async_copy(d_hbm.at[:, at], d_ref.at[:, inner], sems.at[1, part]),
            pltpu.make_async_copy(o_hbm.at[at], o_ref.at[at], sems.at[2, part]),
        ]

    for part in range(len(cuts) - 1):
        for copy in copies(part):
            copy.start()
    table = [t_ref[i] for i in range(3)]
    scale = -spacing / (UNIT * math.log(2.0))

    def tile(t, carry):
        at = pl.ds(pl.multiple_of(t * 8, 8), 8)
        inner = pl.ds(pl.multiple_of(t * 8 + 8, 8), 8)
        for part in range(len(cuts) - 1):

            @pl.when(t * 8 == cuts[part])
            def _(part=part):
                for copy in copies(part):
                    copy.wait()

        for c in range(line // LANES):
            cols = slice(c * LANES, (c + 1) * LANES)
            reverse = o_ref[at, cols] == 1
            passed, colors = [], []
            for k in range(depth):
                *color, extinction = look_up(table, b[k, at, cols])
                passed.append(jnp.exp2(extinction * scale * d_ref[k, inner, cols]))
                colors.append(color)
            t0, t1, t2, t3 = passed
            front, back = t0 * t1, t2 * t3
            ahead = [
                jnp.where(reverse, t1 * back, 1.0),
                jnp.where(reverse, back, t0),
                jnp.where(reverse, t3, front),
                jnp.where(reverse, 1.0, front * t2),
            ]
            for k in range(depth):
                weight = (1.0 - passed[k]) * (1.0 / UNIT) * ahead[k]
                for i in range(3):
                    w_ref[k, i, at, cols] = colors[k][i] * weight
            l_ref[at, cols] = front * back
        return carry

    lax.fori_loop(0, rows // 8, tile, 0)


def look(density, bins, order, table, spacing):
    depth, rows, line = density.shape
    vmem = pl.BlockSpec(memory_space=pltpu.VMEM)
    hbm = pl.BlockSpec(memory_space=pl.ANY)
    cells = depth * rows * line
    return pl.pallas_call(
        lambda *refs: look_kernel(spacing, *refs),
        out_shape=[
            jax.ShapeDtypeStruct((depth, rows + 16, line), F32),
            jax.ShapeDtypeStruct((depth, 3, rows, line), F32),
            jax.ShapeDtypeStruct((rows, line), F32),
            jax.ShapeDtypeStruct((rows, line), jnp.int32),
        ],
        in_specs=[hbm] * 3 + [vmem],
        out_specs=[vmem] * 4,
        scratch_shapes=[
            pltpu.VMEM((depth, rows, line), jnp.int32),
            pltpu.SemaphoreType.DMA((3, 3)),
        ],
        compiler_params=params(12),
        cost_estimate=pl.CostEstimate(
            flops=50 * cells, bytes_accessed=12 * cells, transcendentals=cells
        ),
        name="look",
    )(density, bins, order, table)


def slopes_kernel(d_in, w_ref, ya_ref, yb_ref, d, c_ref, a_ref, n_ref):
    depth, rows, line = d.shape[0], d.shape[1] - 16, d.shape[2]
    chunks = line // LANES
    lat = lax.axis_index("lat")
    lat_odd = (lat & 1) == 1
    keep_low = jnp.where(lat == 0, 0.0, 1.0).astype(F32)
    keep_high = jnp.where(lat == lax.axis_size("lat") - 1, 0.0, 1.0).astype(F32)
    for k in range(depth):
        from_a, from_b = ya_ref[k : k + 1, :], yb_ref[k : k + 1, :]
        d[k, 7:8, :] = jnp.where(lat_odd, from_a, from_b) * keep_low
        d[k, rows + 8 : rows + 9, :] = jnp.where(lat_odd, from_b, from_a) * keep_high
    lane = lax.broadcasted_iota(jnp.int32, (8, LANES), 1)
    sub = lax.broadcasted_iota(jnp.int32, (8, LANES), 0)
    first_lane, last_lane = lane == 0, lane == LANES - 1
    first_sub, last_sub = sub == 0, sub == 7

    def tile(t, carry):
        base = pl.multiple_of(t * 8, 8)
        at = pl.ds(base, 8)
        for c in range(chunks):
            cols = slice(c * LANES, (c + 1) * LANES)

            def cell(k, row, column=c):
                return d[k, pl.ds(row, 8), column * LANES : (column + 1) * LANES]

            total = [None, None, None]
            for k in range(depth):
                here = cell(k, base + 8)
                before, after = cell(k, base), cell(k, base + 16)
                left = cell(k, base + 8, c - 1) if c > 0 else jnp.zeros_like(here)
                right = cell(k, base + 8, c + 1) if c < chunks - 1 else jnp.zeros_like(here)
                step_x = pltpu.roll(jnp.where(first_lane, right, here), LANES - 1, 1) - pltpu.roll(
                    jnp.where(last_lane, left, here), 1, 1
                )
                step_y = pltpu.roll(jnp.where(first_sub, after, here), 7, 0) - pltpu.roll(
                    jnp.where(last_sub, before, here), 1, 0
                )
                tilt = LIGHT_X * step_x + LIGHT_Y * step_y
                norm = step_x * step_x + step_y * step_y + 1.0
                if k in (0, depth - 1):
                    a_ref[min(k, 1), at, cols] = tilt
                    n_ref[min(k, 1), at, cols] = norm
                    continue
                step_z = cell(k + 1, base + 8) - cell(k - 1, base + 8)
                shade = 1.0 + (tilt + LIGHT_Z * step_z) * lax.rsqrt(norm + step_z * step_z)
                for i in range(3):
                    term = w_ref[k, i, at, cols] * shade
                    total[i] = term if total[i] is None else total[i] + term
            for i in range(3):
                c_ref[i, at, cols] = total[i]
        return carry

    lax.fori_loop(0, rows // 8, tile, 0)


def slopes(density, weight, ya, yb):
    depth, rows, line = density.shape
    rows -= 16
    vmem = pl.BlockSpec(memory_space=pltpu.VMEM)
    cells = depth * rows * line
    return pl.pallas_call(
        slopes_kernel,
        out_shape=[
            jax.ShapeDtypeStruct(density.shape, F32),
            jax.ShapeDtypeStruct((3, rows, line), F32),
            jax.ShapeDtypeStruct((2, rows, line), F32),
            jax.ShapeDtypeStruct((2, rows, line), F32),
        ],
        in_specs=[vmem] * 4,
        out_specs=[vmem] * 4,
        input_output_aliases={0: 0},
        compiler_params=params(12),
        cost_estimate=pl.CostEstimate(
            flops=50 * cells, bytes_accessed=12 * cells, transcendentals=cells
        ),
        name="slopes",
    )(density, weight, ya, yb)


def swap_pieces(tiles, sub):
    for size in (4, 2):
        keep = (sub & size) == 0
        step = size // 2
        result = list(tiles)
        for i in range(4):
            if i & step == 0:
                a, b = tiles[i], tiles[i | step]
                result[i] = jnp.where(keep, a, pltpu.roll(b, size, 0))
                result[i | step] = jnp.where(keep, pltpu.roll(a, 8 - size, 0), b)
        tiles = result
    return tiles


def edges_kernel(d_ref, zb_ref, za_ref, o_ref, c_ref, w_ref, l_ref, a_ref, n_ref, *rest):
    outs, mask_ref, s = rest[:8], rest[8], rest[9]
    depth, line = d_ref.shape[0], d_ref.shape[2]
    slab = lax.axis_index("slab")
    slab_odd = (slab & 1) == 1
    keep_low = jnp.where(slab == 0, 0.0, 1.0).astype(F32)
    keep_high = jnp.where(slab == lax.axis_size("slab") - 1, 0.0, 1.0).astype(F32)
    sub = lax.broadcasted_iota(jnp.int32, (8, LANES), 0)
    chunks = line // LANES

    def part(index, carry):
        half, c = index // chunks, index % chunks
        cols = pl.ds(pl.multiple_of(c * LANES, LANES), LANES)
        channels = [[] for _ in range(5)]
        for quarter in range(4):
            at = pl.ds(pl.multiple_of(16 * quarter + 8 * half, 8), 8)
            inner = pl.ds(pl.multiple_of(16 * quarter + 8 * half + 8, 8), 8)
            from_a, from_b = za_ref[at, cols], zb_ref[at, cols]
            below = jnp.where(slab_odd, from_a, from_b) * keep_low
            above = jnp.where(slab_odd, from_b, from_a) * keep_high
            total = [c_ref[i, at, cols] for i in range(3)]
            steps = (d_ref[1, inner, cols] - below, above - d_ref[depth - 2, inner, cols])
            for edge in range(2):
                step_z = steps[edge]
                shade = 1.0 + (a_ref[edge, at, cols] + LIGHT_Z * step_z) * lax.rsqrt(
                    n_ref[edge, at, cols] + step_z * step_z
                )
                for i in range(3):
                    total[i] = total[i] + w_ref[edge * (depth - 1), i, at, cols] * shade
            for i in range(3):
                channels[i].append(total[i])
            channels[3].append(l_ref[at, cols])
            channels[4].append(o_ref[at, cols].astype(F32))
        for i in range(5):
            for piece, value in enumerate(swap_pieces(channels[i], sub)):
                s[4 * half + piece, i, :, cols] = value
        return carry

    lax.fori_loop(0, 2 * chunks, part, 0)
    place = slab & 7
    for j in range(8):
        for i in range(4):
            outs[j][i] = s[place ^ j, i]
    mask_ref[...] = s[place, 4]


def edges(density, za, zb, order, color, weight, light, tilt, norm):
    depth, rows, line = density.shape
    rows -= 16
    vmem = pl.BlockSpec(memory_space=pltpu.VMEM)
    return pl.pallas_call(
        edges_kernel,
        out_shape=[jax.ShapeDtypeStruct((4, 8, line), F32)] * 8
        + [jax.ShapeDtypeStruct((8, line), F32)],
        in_specs=[vmem] * 9,
        out_specs=[vmem] * 9,
        scratch_shapes=[pltpu.VMEM((8, 5, 8, line), F32)],
        compiler_params=params(12),
        cost_estimate=pl.CostEstimate(
            flops=40 * depth * rows * line, bytes_accessed=4 * depth * rows * line, transcendentals=depth * rows * line
        ),
        name="edges",
    )(density, zb, za, order, color, weight, light, tilt, norm)


def merge(a, b, b_first):
    front = [jnp.where(b_first, y, x) for x, y in zip(a, b)]
    back = [jnp.where(b_first, x, y) for x, y in zip(a, b)]
    return [front[i] + front[3] * back[i] for i in range(3)] + [front[3] * back[3]]


def merge_tree(blocks, mask, place):
    bit = 0
    while len(blocks) > 1:
        b_first = jnp.logical_xor(mask > 0.5, (place >> bit & 1) == 1)
        blocks = [merge(blocks[i], blocks[i + 1], b_first) for i in range(0, len(blocks), 2)]
        bit += 1
    return blocks[0]


def eight_kernel(*refs):
    ins, mask_ref, outs, own_mask = refs[:8], refs[8], refs[9:13], refs[13]
    line = mask_ref.shape[1]
    slab = lax.axis_index("slab")
    place, quarter = slab & 7, slab >> 3
    sub = lax.broadcasted_iota(jnp.int32, (8, LANES), 0) // 2

    def part(c, carry):
        cols = pl.ds(pl.multiple_of(c * LANES, LANES), LANES)
        mask = mask_ref[:, cols]
        blocks = [[ins[ORDER8.index(j)][i, :, cols] for i in range(4)] for j in range(8)]
        merged = merge_tree(blocks, mask, place)
        for j in range(4):
            target = quarter ^ j
            packed = None
            for i in range(4):
                moved = pltpu.roll(merged[i], (2 * i + 8 - 2 * target) & 7, 0)
                packed = moved if packed is None else jnp.where(sub == i, moved, packed)
            outs[j][:, cols] = packed
        own_mask[:, cols] = pltpu.roll(mask, (8 - 2 * quarter) & 7, 0)
        return carry

    lax.fori_loop(0, line // LANES, part, 0)


def merge_eight(blocks, mask):
    line = mask.shape[1]
    vmem = pl.BlockSpec(memory_space=pltpu.VMEM)
    return pl.pallas_call(
        eight_kernel,
        out_shape=[jax.ShapeDtypeStruct((8, line), F32)] * 5,
        in_specs=[vmem] * 9,
        out_specs=[vmem] * 5,
        compiler_params=params(6),
        name="merge_eight",
    )(*[blocks[j] for j in ORDER8], mask)


def four_kernel(*refs):
    ins, mask_ref, out = refs[:4], refs[4], refs[5]
    place = lax.axis_index("slab") >> 3
    mask = mask_ref[0:2, :]
    blocks = [[ins[ORDER4.index(j)][2 * i : 2 * i + 2, :] for i in range(4)] for j in range(4)]
    merged = merge_tree(blocks, mask, place)
    for i in range(3):
        out[i] = merged[i]
    out[3] = 1.0 - merged[3]


def merge_four(blocks, mask):
    line = mask.shape[1]
    vmem = pl.BlockSpec(memory_space=pltpu.VMEM)
    return pl.pallas_call(
        four_kernel,
        out_shape=jax.ShapeDtypeStruct((4, 2, line), F32),
        in_specs=[vmem] * 5,
        out_specs=vmem,
        compiler_params=params(4),
        name="merge_four",
    )(*[blocks[j] for j in ORDER4], mask)


def swap(block, axis, step):
    count = lax.axis_size(axis)
    return lax.ppermute(block, axis, [(i, i ^ step) for i in range(count)])


def swap_odd(block, axis):
    slabs, lats = lax.axis_size("slab"), lax.axis_size("lat")
    route = []
    for slab in range(slabs):
        for lat in range(lats):
            at, count = (slab, slabs) if axis == "slab" else (lat, lats)
            step = 2 * (at & 1) - 1
            if at in (0, count - 1):
                partner = (slab, lat ^ 1) if axis == "slab" else (slab ^ 1, lat)
            else:
                partner = (slab + step, lat) if axis == "slab" else (slab, lat + step)
            route.append((slab * lats + lat, partner[0] * lats + partner[1]))
    return lax.ppermute(block, ("slab", "lat"), route)


def shards(density, bins, transfer, depth_order):
    depth_cells = density.shape[0]
    spacing = 1.5 / (depth_cells * lax.axis_size("slab"))
    density, bins, transfer, depth_order = (
        pltpu.with_memory_space_constraint(x, pltpu.HBM)
        for x in (density, bins, transfer, depth_order)
    )
    za, zb, ya, yb, table = faces(density, transfer)
    za, zb = swap(za, "slab", 1), swap_odd(zb, "slab")
    ya, yb = swap(ya, "lat", 1), swap_odd(yb, "lat")
    density, weight, light, order = look(density, bins, depth_order, table, spacing)
    density, color, tilt, norm = slopes(density, weight, ya, yb)
    *blocks, mask = edges(density, za, zb, order, color, weight, light, tilt, norm)
    blocks = blocks[:1] + [swap(blocks[j], "slab", j) for j in range(1, 8)]
    *quarters, mask = merge_eight(blocks, mask)
    quarters = quarters[:1] + [swap(quarters[j], "slab", 8 * j) for j in range(1, 4)]
    return merge_four(quarters, mask)


def solution(mesh):
    return jax.shard_map(
        shards,
        mesh=mesh,
        in_specs=(P("slab", "lat", None), P("slab", "lat", None), P(), P("lat", None)),
        out_specs=P(None, ("lat", "slab"), None),
        check_vma=False,
    )
```

```python
import math

import jax
import jax.numpy as jnp
from jax import lax
from jax.experimental import pallas as pl
from jax.experimental.pallas import tpu as pltpu
from jax.sharding import PartitionSpec as P

LIGHT_X = 0.48
LIGHT_Y = 0.6
LIGHT_Z = 0.64
UNIT = 2048.0
LANES = 128
MIB = 1024 * 1024
F32 = jnp.float32
ORDER8 = (1, 7, 3, 5, 2, 6, 4, 0)
ORDER4 = (2, 3, 1, 0)


def params(mib):
    return pltpu.CompilerParams(vmem_limit_bytes=mib * MIB)


def faces_kernel(d_ref, t_ref, za_ref, zb_ref, ya_ref, yb_ref, table_ref, low, high, t, sems):
    depth, rows = d_ref.shape[0], d_ref.shape[1]
    slab_odd = lax.axis_index("slab") & 1
    lat_odd = lax.axis_index("lat") & 1
    last = depth - 1
    copies = [
        pltpu.make_async_copy(d_ref.at[last - last * slab_odd], za_ref, sems.at[0]),
        pltpu.make_async_copy(d_ref.at[last * slab_odd], zb_ref, sems.at[1]),
        pltpu.make_async_copy(d_ref.at[:, pl.ds(0, 8)], low, sems.at[2]),
        pltpu.make_async_copy(d_ref.at[:, pl.ds(rows - 8, 8)], high, sems.at[3]),
        pltpu.make_async_copy(t_ref, t, sems.at[4]),
    ]
    for copy in copies:
        copy.start()
    copies[4].wait()
    units = (t[...].astype(F32) * UNIT).astype(jnp.int32)
    red, green, blue, extinction = (units[i : i + 1] for i in range(4))
    word = red | (green << 12) | (blue << 24)
    rest = extinction | ((blue >> 8) << 12)
    halves = slice(0, LANES), slice(LANES, 2 * LANES)
    parts = [word[:, half] for half in halves] + [rest[:, halves[0]] | (rest[:, halves[1]] << 16)]
    for i, part in enumerate(parts):
        table_ref[i] = jnp.broadcast_to(part, (8, LANES))
    copies[2].wait()
    copies[3].wait()
    odd = lat_odd == 1
    for k in range(depth):
        first, final = low[k, 0:1], high[k, 7:8]
        ya_ref[k : k + 1, :] = jnp.where(odd, first, final)
        yb_ref[k : k + 1, :] = jnp.where(odd, final, first)
    copies[0].wait()
    copies[1].wait()


def faces(density, transfer):
    depth, rows, line = density.shape
    return pl.pallas_call(
        faces_kernel,
        out_shape=[
            jax.ShapeDtypeStruct((rows, line), F32),
            jax.ShapeDtypeStruct((rows, line), F32),
            jax.ShapeDtypeStruct((depth, line), F32),
            jax.ShapeDtypeStruct((depth, line), F32),
            jax.ShapeDtypeStruct((3, 8, LANES), jnp.int32),
        ],
        in_specs=[pl.BlockSpec(memory_space=pl.ANY)] * 2,
        out_specs=[pl.BlockSpec(memory_space=pl.ANY)] * 2
        + [pl.BlockSpec(memory_space=pltpu.VMEM)] * 3,
        scratch_shapes=[
            pltpu.VMEM((depth, 8, line), F32),
            pltpu.VMEM((depth, 8, line), F32),
            pltpu.VMEM(transfer.shape, transfer.dtype),
            pltpu.SemaphoreType.DMA((5,)),
        ],
        compiler_params=params(4),
        name="faces",
    )(density, transfer)


def columns_of(table, column):
    numbers = lax.GatherDimensionNumbers(
        offset_dims=(),
        collapsed_slice_dims=(1,),
        start_index_map=(1,),
        operand_batching_dims=(0,),
        start_indices_batching_dims=(0,),
    )
    return lax.gather(
        table, column[..., None], numbers, (1, 1), mode=lax.GatherScatterMode.PROMISE_IN_BOUNDS
    )


def look_up(table, bins):
    column = bins & (LANES - 1)
    upper = bins >= LANES
    low_half, high_half, rest = (columns_of(part, column) for part in table)
    word = jnp.where(upper, high_half, low_half)
    rest = jnp.where(upper, rest >> 16, rest)
    blue = ((rest >> 4) & 0xF00) | lax.shift_right_logical(word, 24)
    units = (word & 0xFFF, (word >> 12) & 0xFFF, blue, rest & 0xFFF)
    return [value.astype(F32) for value in units]


def look_kernel(spacing, d_hbm, b_hbm, o_hbm, t_ref, d_ref, w_ref, l_ref, o_ref, b, sems):
    depth, rows, line = d_hbm.shape

    cuts = (0, 8, 32, rows)

    def copies(part):
        first, size = cuts[part], cuts[part + 1] - cuts[part]
        at, inner = pl.ds(first, size), pl.ds(first + 8, size)
        return [
            pltpu.make_async_copy(b_hbm.at[:, at], b.at[:, at], sems.at[0, part]),
            pltpu.make_async_copy(d_hbm.at[:, at], d_ref.at[:, inner], sems.at[1, part]),
            pltpu.make_async_copy(o_hbm.at[at], o_ref.at[at], sems.at[2, part]),
        ]

    for part in range(len(cuts) - 1):
        for copy in copies(part):
            copy.start()
    table = [t_ref[i] for i in range(3)]
    scale = -spacing / (UNIT * math.log(2.0))

    def tile(t, carry):
        at = pl.ds(pl.multiple_of(t * 8, 8), 8)
        inner = pl.ds(pl.multiple_of(t * 8 + 8, 8), 8)
        for part in range(len(cuts) - 1):

            @pl.when(t * 8 == cuts[part])
            def _(part=part):
                for copy in copies(part):
                    copy.wait()

        for c in range(line // LANES):
            cols = slice(c * LANES, (c + 1) * LANES)
            reverse = o_ref[at, cols] == 1
            passed, colors = [], []
            for k in range(depth):
                *color, extinction = look_up(table, b[k, at, cols])
                passed.append(jnp.exp2(extinction * scale * d_ref[k, inner, cols]))
                colors.append(color)
            t0, t1, t2, t3 = passed
            front, back = t0 * t1, t2 * t3
            ahead = [
                jnp.where(reverse, t1 * back, 1.0),
                jnp.where(reverse, back, t0),
                jnp.where(reverse, t3, front),
                jnp.where(reverse, 1.0, front * t2),
            ]
            for k in range(depth):
                weight = (1.0 - passed[k]) * (1.0 / UNIT) * ahead[k]
                for i in range(3):
                    w_ref[k, i, at, cols] = colors[k][i] * weight
            l_ref[at, cols] = front * back
        return carry

    lax.fori_loop(0, rows // 8, tile, 0)


def look(density, bins, order, table, spacing):
    depth, rows, line = density.shape
    vmem = pl.BlockSpec(memory_space=pltpu.VMEM)
    hbm = pl.BlockSpec(memory_space=pl.ANY)
    cells = depth * rows * line
    return pl.pallas_call(
        lambda *refs: look_kernel(spacing, *refs),
        out_shape=[
            jax.ShapeDtypeStruct((depth, rows + 16, line), F32),
            jax.ShapeDtypeStruct((depth, 3, rows, line), F32),
            jax.ShapeDtypeStruct((rows, line), F32),
            jax.ShapeDtypeStruct((rows, line), jnp.int32),
        ],
        in_specs=[hbm] * 3 + [vmem],
        out_specs=[vmem] * 4,
        scratch_shapes=[
            pltpu.VMEM((depth, rows, line), jnp.int32),
            pltpu.SemaphoreType.DMA((3, 3)),
        ],
        compiler_params=params(12),
        cost_estimate=pl.CostEstimate(
            flops=50 * cells, bytes_accessed=12 * cells, transcendentals=cells
        ),
        name="look",
    )(density, bins, order, table)


def slopes_kernel(d_in, w_ref, ya_ref, yb_ref, d, c_ref, a_ref, n_ref):
    depth, rows, line = d.shape[0], d.shape[1] - 16, d.shape[2]
    chunks = line // LANES
    lat = lax.axis_index("lat")
    lat_odd = (lat & 1) == 1
    keep_low = jnp.where(lat == 0, 0.0, 1.0).astype(F32)
    keep_high = jnp.where(lat == lax.axis_size("lat") - 1, 0.0, 1.0).astype(F32)
    for k in range(depth):
        from_a, from_b = ya_ref[k : k + 1, :], yb_ref[k : k + 1, :]
        d[k, 7:8, :] = jnp.where(lat_odd, from_a, from_b) * keep_low
        d[k, rows + 8 : rows + 9, :] = jnp.where(lat_odd, from_b, from_a) * keep_high
    lane = lax.broadcasted_iota(jnp.int32, (8, LANES), 1)
    sub = lax.broadcasted_iota(jnp.int32, (8, LANES), 0)
    first_lane, last_lane = lane == 0, lane == LANES - 1
    first_sub, last_sub = sub == 0, sub == 7

    def tile(t, carry):
        base = pl.multiple_of(t * 8, 8)
        at = pl.ds(base, 8)
        for c in range(chunks):
            cols = slice(c * LANES, (c + 1) * LANES)

            def cell(k, row, column=c):
                return d[k, pl.ds(row, 8), column * LANES : (column + 1) * LANES]

            total = [None, None, None]
            for k in range(depth):
                here = cell(k, base + 8)
                before, after = cell(k, base), cell(k, base + 16)
                left = cell(k, base + 8, c - 1) if c > 0 else jnp.zeros_like(here)
                right = cell(k, base + 8, c + 1) if c < chunks - 1 else jnp.zeros_like(here)
                step_x = pltpu.roll(jnp.where(first_lane, right, here), LANES - 1, 1) - pltpu.roll(
                    jnp.where(last_lane, left, here), 1, 1
                )
                step_y = pltpu.roll(jnp.where(first_sub, after, here), 7, 0) - pltpu.roll(
                    jnp.where(last_sub, before, here), 1, 0
                )
                tilt = LIGHT_X * step_x + LIGHT_Y * step_y
                norm = step_x * step_x + step_y * step_y + 1.0
                if k in (0, depth - 1):
                    a_ref[min(k, 1), at, cols] = tilt
                    n_ref[min(k, 1), at, cols] = norm
                    continue
                step_z = cell(k + 1, base + 8) - cell(k - 1, base + 8)
                shade = 1.0 + (tilt + LIGHT_Z * step_z) * lax.rsqrt(norm + step_z * step_z)
                for i in range(3):
                    term = w_ref[k, i, at, cols] * shade
                    total[i] = term if total[i] is None else total[i] + term
            for i in range(3):
                c_ref[i, at, cols] = total[i]
        return carry

    lax.fori_loop(0, rows // 8, tile, 0)


def slopes(density, weight, ya, yb):
    depth, rows, line = density.shape
    rows -= 16
    vmem = pl.BlockSpec(memory_space=pltpu.VMEM)
    cells = depth * rows * line
    return pl.pallas_call(
        slopes_kernel,
        out_shape=[
            jax.ShapeDtypeStruct(density.shape, F32),
            jax.ShapeDtypeStruct((3, rows, line), F32),
            jax.ShapeDtypeStruct((2, rows, line), F32),
            jax.ShapeDtypeStruct((2, rows, line), F32),
        ],
        in_specs=[vmem] * 4,
        out_specs=[vmem] * 4,
        input_output_aliases={0: 0},
        compiler_params=params(12),
        cost_estimate=pl.CostEstimate(
            flops=50 * cells, bytes_accessed=12 * cells, transcendentals=cells
        ),
        name="slopes",
    )(density, weight, ya, yb)


def swap_pieces(tiles, sub):
    for size in (4, 2):
        keep = (sub & size) == 0
        step = size // 2
        result = list(tiles)
        for i in range(4):
            if i & step == 0:
                a, b = tiles[i], tiles[i | step]
                result[i] = jnp.where(keep, a, pltpu.roll(b, size, 0))
                result[i | step] = jnp.where(keep, pltpu.roll(a, 8 - size, 0), b)
        tiles = result
    return tiles


def edges_kernel(d_ref, zb_ref, za_ref, o_ref, c_ref, w_ref, l_ref, a_ref, n_ref, *rest):
    outs, mask_ref, s = rest[:8], rest[8], rest[9]
    depth, line = d_ref.shape[0], d_ref.shape[2]
    slab = lax.axis_index("slab")
    slab_odd = (slab & 1) == 1
    keep_low = jnp.where(slab == 0, 0.0, 1.0).astype(F32)
    keep_high = jnp.where(slab == lax.axis_size("slab") - 1, 0.0, 1.0).astype(F32)
    sub = lax.broadcasted_iota(jnp.int32, (8, LANES), 0)
    chunks = line // LANES

    def part(index, carry):
        half, c = index // chunks, index % chunks
        cols = pl.ds(pl.multiple_of(c * LANES, LANES), LANES)
        channels = [[] for _ in range(5)]
        for quarter in range(4):
            at = pl.ds(pl.multiple_of(16 * quarter + 8 * half, 8), 8)
            inner = pl.ds(pl.multiple_of(16 * quarter + 8 * half + 8, 8), 8)
            from_a, from_b = za_ref[at, cols], zb_ref[at, cols]
            below = jnp.where(slab_odd, from_a, from_b) * keep_low
            above = jnp.where(slab_odd, from_b, from_a) * keep_high
            total = [c_ref[i, at, cols] for i in range(3)]
            steps = (d_ref[1, inner, cols] - below, above - d_ref[depth - 2, inner, cols])
            for edge in range(2):
                step_z = steps[edge]
                shade = 1.0 + (a_ref[edge, at, cols] + LIGHT_Z * step_z) * lax.rsqrt(
                    n_ref[edge, at, cols] + step_z * step_z
                )
                for i in range(3):
                    total[i] = total[i] + w_ref[edge * (depth - 1), i, at, cols] * shade
            for i in range(3):
                channels[i].append(total[i])
            channels[3].append(l_ref[at, cols])
            channels[4].append(o_ref[at, cols].astype(F32))
        for i in range(5):
            for piece, value in enumerate(swap_pieces(channels[i], sub)):
                s[4 * half + piece, i, :, cols] = value
        return carry

    lax.fori_loop(0, 2 * chunks, part, 0, unroll=2)
    place = slab & 7
    for j in range(8):
        for i in range(4):
            outs[j][i] = s[place ^ j, i]
    mask_ref[...] = s[place, 4]


def edges(density, za, zb, order, color, weight, light, tilt, norm):
    depth, rows, line = density.shape
    rows -= 16
    vmem = pl.BlockSpec(memory_space=pltpu.VMEM)
    return pl.pallas_call(
        edges_kernel,
        out_shape=[jax.ShapeDtypeStruct((4, 8, line), F32)] * 8
        + [jax.ShapeDtypeStruct((8, line), F32)],
        in_specs=[vmem] * 9,
        out_specs=[vmem] * 9,
        scratch_shapes=[pltpu.VMEM((8, 5, 8, line), F32)],
        compiler_params=params(12),
        cost_estimate=pl.CostEstimate(
            flops=40 * depth * rows * line, bytes_accessed=4 * depth * rows * line, transcendentals=depth * rows * line
        ),
        name="edges",
    )(density, zb, za, order, color, weight, light, tilt, norm)


def merge(a, b, b_first):
    front = [jnp.where(b_first, y, x) for x, y in zip(a, b)]
    back = [jnp.where(b_first, x, y) for x, y in zip(a, b)]
    return [front[i] + front[3] * back[i] for i in range(3)] + [front[3] * back[3]]


def merge_tree(blocks, mask, place):
    bit = 0
    while len(blocks) > 1:
        b_first = jnp.logical_xor(mask > 0.5, (place >> bit & 1) == 1)
        blocks = [merge(blocks[i], blocks[i + 1], b_first) for i in range(0, len(blocks), 2)]
        bit += 1
    return blocks[0]


def eight_kernel(*refs):
    ins, mask_ref, outs, own_mask = refs[:8], refs[8], refs[9:13], refs[13]
    line = mask_ref.shape[1]
    slab = lax.axis_index("slab")
    place, quarter = slab & 7, slab >> 3
    sub = lax.broadcasted_iota(jnp.int32, (8, LANES), 0) // 2

    def part(c, carry):
        cols = pl.ds(pl.multiple_of(c * LANES, LANES), LANES)
        mask = mask_ref[:, cols]
        blocks = [[ins[ORDER8.index(j)][i, :, cols] for i in range(4)] for j in range(8)]
        merged = merge_tree(blocks, mask, place)
        for j in range(4):
            target = quarter ^ j
            packed = None
            for i in range(4):
                moved = pltpu.roll(merged[i], (2 * i + 8 - 2 * target) & 7, 0)
                packed = moved if packed is None else jnp.where(sub == i, moved, packed)
            outs[j][:, cols] = packed
        own_mask[:, cols] = pltpu.roll(mask, (8 - 2 * quarter) & 7, 0)
        return carry

    lax.fori_loop(0, line // LANES, part, 0)


def merge_eight(blocks, mask):
    line = mask.shape[1]
    vmem = pl.BlockSpec(memory_space=pltpu.VMEM)
    return pl.pallas_call(
        eight_kernel,
        out_shape=[jax.ShapeDtypeStruct((8, line), F32)] * 5,
        in_specs=[vmem] * 9,
        out_specs=[vmem] * 5,
        compiler_params=params(6),
        name="merge_eight",
    )(*[blocks[j] for j in ORDER8], mask)


def four_kernel(*refs):
    ins, mask_ref, out = refs[:4], refs[4], refs[5]
    place = lax.axis_index("slab") >> 3
    mask = mask_ref[0:2, :]
    blocks = [[ins[ORDER4.index(j)][2 * i : 2 * i + 2, :] for i in range(4)] for j in range(4)]
    merged = merge_tree(blocks, mask, place)
    for i in range(3):
        out[i] = merged[i]
    out[3] = 1.0 - merged[3]


def merge_four(blocks, mask):
    line = mask.shape[1]
    vmem = pl.BlockSpec(memory_space=pltpu.VMEM)
    return pl.pallas_call(
        four_kernel,
        out_shape=jax.ShapeDtypeStruct((4, 2, line), F32),
        in_specs=[vmem] * 5,
        out_specs=vmem,
        compiler_params=params(4),
        name="merge_four",
    )(*[blocks[j] for j in ORDER4], mask)


def swap(block, axis, step):
    count = lax.axis_size(axis)
    return lax.ppermute(block, axis, [(i, i ^ step) for i in range(count)])


def swap_odd(block, axis):
    slabs, lats = lax.axis_size("slab"), lax.axis_size("lat")
    route = []
    for slab in range(slabs):
        for lat in range(lats):
            at, count = (slab, slabs) if axis == "slab" else (lat, lats)
            step = 2 * (at & 1) - 1
            if at in (0, count - 1):
                partner = (slab, lat ^ 1) if axis == "slab" else (slab ^ 1, lat)
            else:
                partner = (slab + step, lat) if axis == "slab" else (slab, lat + step)
            route.append((slab * lats + lat, partner[0] * lats + partner[1]))
    return lax.ppermute(block, ("slab", "lat"), route)


def shards(density, bins, transfer, depth_order):
    depth_cells = density.shape[0]
    spacing = 1.5 / (depth_cells * lax.axis_size("slab"))
    density, bins, transfer, depth_order = (
        pltpu.with_memory_space_constraint(x, pltpu.HBM)
        for x in (density, bins, transfer, depth_order)
    )
    za, zb, ya, yb, table = faces(density, transfer)
    za, zb = swap(za, "slab", 1), swap_odd(zb, "slab")
    ya, yb = swap(ya, "lat", 1), swap_odd(yb, "lat")
    density, weight, light, order = look(density, bins, depth_order, table, spacing)
    density, color, tilt, norm = slopes(density, weight, ya, yb)
    *blocks, mask = edges(density, za, zb, order, color, weight, light, tilt, norm)
    blocks = blocks[:1] + [swap(blocks[j], "slab", j) for j in range(1, 8)]
    *quarters, mask = merge_eight(blocks, mask)
    quarters = quarters[:1] + [swap(quarters[j], "slab", 8 * j) for j in range(1, 4)]
    return merge_four(quarters, mask)


def solution(mesh):
    return jax.shard_map(
        shards,
        mesh=mesh,
        in_specs=(P("slab", "lat", None), P("slab", "lat", None), P(), P("lat", None)),
        out_specs=P(None, ("lat", "slab"), None),
        check_vma=False,
    )
```
